128 devices in a mesh: group: 2 (over core), fsdp: 8 (over x, y_hi), tp: 8 (over z, y_lo).
Axes of the slice: x: 4, y: 4 (y_hi: 2, y_lo: 2; y = y_hi * 2 + y_lo), z: 4, core: 2. Of those that a mesh axis runs over, the one named last changes fastest.
Arguments:
- learn_input: bfloat16 [16384, 5120], P(('group', 'fsdp')), may hold values from -8 to 8
- learn_cotangent: bfloat16 [16384, 2, 1024], P(('group', 'fsdp'), None, 'tp'), may hold values from -0.375 to 0.375
- weight: float32 [5120, 2, 1024], P(('group', 'fsdp'), None, 'tp'), may hold values from -0.078125 to 0.078125
- moment: float32 [5120, 2, 1024], P(('group', 'fsdp'), None, 'tp'), may hold values from -6 to 6
- second: float32 [5120, 2, 1024], P(('group', 'fsdp'), None, 'tp'), may hold values from 1 to 10
- table: bfloat16 [77824, 5120], P(('group', 'fsdp'), 'tp'), may hold values from -6 to 6
- gain: bfloat16 [5120], replicated, may hold values from 0.099609375 to 1.8984375
- query_weight: bfloat16 [5120, 8192], P(None, 'tp'), may hold values from -0.078125 to 0.078125
- cache: bfloat16 [2, 32, 8, 4096, 128], P(None, ('group', 'fsdp'), 'tp'), may hold values from -6 to 6
- token_ids: int32 [32, 3], replicated, may hold values from 0 to 77823
- lengths: int32 [32], P(('group', 'fsdp')), may hold values from 1 to 4096
Outputs:
- new_weight: float32 [5120, 2, 1024], P(('group', 'fsdp'), None, 'tp')
- new_moment: float32 [5120, 2, 1024], P(('group', 'fsdp'), None, 'tp')
- new_second: float32 [5120, 2, 1024], P(('group', 'fsdp'), None, 'tp')
- new_kv: bfloat16 [2, 32, 8, 3, 128], P(None, ('group', 'fsdp'), 'tp')
- attended: bfloat16 [32, 3, 8192], P(('group', 'fsdp'), None, 'tp')
The draws below stay inside these ranges and needn't reach their ends.
All inputs are finite; a program needn't handle non-finite values.
Results may differ from the reference program's by a relative error of at most 0.02.
Values may be sent and summed in bfloat16 or wider, within the bound.
A program may use at most 128 MiB of HBM per device.

```python
import math
import jax
import jax.numpy as jnp
from jax import lax

MODEL_WIDTH = 5120
QUERY_HEADS = 64
KEY_VALUE_HEADS = 8
HEAD_SIZE = 128
DECODE_STEPS = 3
TOK_DEV = 1024
CACHE_POSITIONS = 4096
KEY_FEATURES = 1024
QD = 8192
TOKENS = 16384
DECODE_ROWS = 32
VOCAB = 77824
N_GROUP = 2
N_FSDP = 8


def with_ends(array, own_key, low, largest):
    longest = array.shape.index(max(array.shape))
    spots = []
    for shift in (0, 1):
        where = [jax.random.randint(jax.random.fold_in(own_key, axis), (), 0, length) for axis, length in enumerate(array.shape)]
        where[longest] = (where[longest] + shift) % array.shape[longest]
        spots.append(tuple(where))
    return array.at[spots[0]].set(low).at[spots[1]].set(largest)


def strengthened(values, own_key, source, target, parts, factor):
    owner, partner = [(jnp.arange(values.shape[position]) // (values.shape[position] // parts)).reshape([-1 if axis == position else 1 for axis in range(values.ndim)]) for position in (source, target)]
    chosen = jax.random.permutation(own_key, parts)[partner]
    strong = (owner == chosen) | (owner == (partner + parts // 2) % parts)
    return jnp.where(strong, factor * values, values)


def steps_of(rng, shape, pieces, least, largest):
    loudness, own = 1.0, jax.random.fold_in(rng, 6)
    for axis_at, blocks in pieces:
        draws = jnp.exp(jax.random.uniform(jax.random.fold_in(own, axis_at), (blocks,), jnp.float32, least / len(pieces), largest / len(pieces)))
        loudness = loudness * jnp.repeat(draws, shape[axis_at] // blocks).reshape([-1 if axis == axis_at else 1 for axis in range(len(shape))])
    return loudness


def centred(own_key, extent, width, limit, pieces=(), kind=jnp.bfloat16):
    level = steps_of(own_key, extent, pieces, -0.22, 0.18) if pieces else 1.0
    entries = jax.random.normal(own_key, extent, jnp.float32) * width * level
    return jnp.minimum(jnp.maximum(entries, -limit), limit).astype(kind)


def gaussian_with(stream_key, extent, spread, limit, cuts, heavy, held_as=jnp.bfloat16):
    array = spread * jax.random.normal(stream_key, extent, jnp.float32)
    if cuts:
        array = array * steps_of(stream_key, extent, cuts, -0.22, 0.18)
    return jnp.clip(strengthened(array, jax.random.fold_in(stream_key, 3), *heavy), -limit, limit).astype(held_as)


def setup_inputs(seed: int = 0) -> dict:
    splits = jax.random.split(jax.random.key(seed), 12)
    return {
        "learn_input": gaussian_with(splits[0], (TOKENS, MODEL_WIDTH), 1.0, 8.0, ((0, 16),), (0, 1, 16, 2.0)),
        "learn_cotangent": centred(splits[1], (TOKENS, 2, KEY_FEATURES), (2.0 / TOK_DEV ** 0.5), 0.375, ((0, 16), (2, 8))),
        "weight": centred(splits[2], (MODEL_WIDTH, 2, KEY_FEATURES), MODEL_WIDTH ** -0.5, 0.078125, ((0, 16), (2, 8)), jnp.float32),
        "moment": centred(splits[3], (MODEL_WIDTH, 2, KEY_FEATURES), 1.0, 6.0, ((0, 16), (2, 8)), jnp.float32),
        "second": jnp.clip(jnp.exp(math.log(10.0) - 2.3025851 * jax.random.uniform(splits[4], (MODEL_WIDTH, 2, KEY_FEATURES), jnp.float32) ** steps_of(splits[4], (MODEL_WIDTH, 2, KEY_FEATURES), ((0, 16), (2, 8)), -0.2, 0.2)), 1.0, 10.0),
        "table": centred(splits[5], (VOCAB, MODEL_WIDTH), 1.0, 6.0, ((0, 16), (1, 8))),
        "gain": jnp.clip(1.0 + 0.18 * jax.random.normal(splits[6], (MODEL_WIDTH,), jnp.float32), 0.099609375, 1.8984375).astype(jnp.bfloat16),
        "query_weight": centred(splits[7], (MODEL_WIDTH, QD), MODEL_WIDTH ** -0.5, 0.078125, ((1, 8),)),
        "cache": centred(splits[8], (2, DECODE_ROWS, KEY_VALUE_HEADS, CACHE_POSITIONS, HEAD_SIZE), 1.0, 6.0, ((1, 16), (2, 8))),
        "token_ids": with_ends(jax.random.randint(splits[9], (DECODE_ROWS, DECODE_STEPS), 0, VOCAB), jax.random.fold_in(splits[9], 1), 0, VOCAB - 1).astype(jnp.int32),
        "lengths": with_ends(jax.random.randint(splits[10], (DECODE_ROWS,), 1, CACHE_POSITIONS + 1), jax.random.fold_in(splits[10], 1), 1, CACHE_POSITIONS).astype(jnp.int32),
    }


learn_rate = 0.002
beta_one = 0.9
beta_two = 0.95
bias_one = 1.0 - 0.9 ** 10
bias_two = 1.0 - 0.95 ** 10
adam_eps = 1e-08
weight_decay = 0.1
norm_eps = 1e-06
rope_log = math.log(1000000.0)

def head_norm(values):
    return values * lax.rsqrt(lax.optimization_barrier(jnp.mean(values * values, axis=-1, keepdims=True)) + norm_eps)

def rotate(values, positions):
    half = values.shape[-1] // 2
    freqs = jnp.exp(-rope_log * 2.0 * jnp.arange(half, dtype=jnp.float32) / values.shape[-1])
    angles = positions.astype(jnp.float32)[:, :, None, None] * freqs
    cosine = jnp.cos(angles)
    sine = jnp.sin(angles)
    first = values[..., :half]
    latter = values[..., half:]
    return jnp.concatenate([first * cosine - latter * sine, latter * cosine + first * sine], axis=-1)

def attend_row(query_vectors, old_keys, old_values, new_keys, new_values, length):
    scale = 1.0 / math.sqrt(query_vectors.shape[-1])
    query32 = query_vectors.astype(jnp.float32)
    old = jnp.einsum('skgd,kcd->skgc', query32, old_keys.astype(jnp.float32)) * scale
    live = jnp.arange(old_keys.shape[1]) < length
    old_w = jnp.where(live, jnp.exp(old), 0.0)
    fresh_weights = jnp.einsum('skgd,tkd->skgt', query32, new_keys.astype(jnp.float32)) * scale
    steps = query_vectors.shape[0]
    causal = jnp.arange(steps)[:, None] >= jnp.arange(steps)[None, :]
    fresh_w = jnp.where(causal[:, None, None, :], jnp.exp(fresh_weights), 0.0)
    denom = lax.optimization_barrier(jnp.sum(old_w, axis=-1)) + lax.optimization_barrier(jnp.sum(fresh_w, axis=-1))
    numer = jnp.einsum('skgc,kcd->skgd', old_w.astype(jnp.bfloat16).astype(jnp.float32), old_values.astype(jnp.float32))
    numer = numer + jnp.einsum('skgt,tkd->skgd', fresh_w.astype(jnp.bfloat16).astype(jnp.float32), new_values.astype(jnp.float32))
    return (numer / denom[..., None]).astype(jnp.bfloat16)

def reference(learn_input, learn_cotangent, weight, moment, second, table, gain, query_weight, cache, token_ids, lengths):
    blocks = N_GROUP * N_FSDP
    input_blocks = learn_input.reshape(blocks, TOK_DEV, MODEL_WIDTH)
    cot_blocks = learn_cotangent.reshape(blocks, TOK_DEV, 2 * KEY_FEATURES)

    def add_block(total, items):
        block_in, block_cot = items
        term = jnp.dot(block_in.T, block_cot, preferred_element_type=jnp.float32)
        return (total + term.astype(jnp.bfloat16).astype(jnp.float32), None)
    grad, _ = lax.scan(add_block, jnp.zeros((MODEL_WIDTH, 2 * KEY_FEATURES), jnp.float32), (input_blocks, cot_blocks))
    grad = grad.reshape(MODEL_WIDTH, 2, KEY_FEATURES)
    new_moment = beta_one * moment + (1.0 - beta_one) * grad
    new_second = beta_two * second + (1.0 - beta_two) * grad * grad
    update = new_moment / bias_one / (jnp.sqrt(new_second / bias_two) + adam_eps)
    new_weight = weight - learn_rate * (update + weight_decay * weight)
    fresh_weights = new_weight.astype(jnp.bfloat16)
    emb = jnp.take(table, token_ids, axis=0).astype(jnp.float32)
    mean_sq = lax.optimization_barrier(jnp.mean(emb * emb, axis=-1, keepdims=True))
    normed = (emb * gain.astype(jnp.float32) * lax.rsqrt(mean_sq + norm_eps)).astype(jnp.bfloat16)
    flat_layout = normed.reshape(DECODE_ROWS * DECODE_STEPS, MODEL_WIDTH)
    qraw = jnp.dot(flat_layout, query_weight, preferred_element_type=jnp.float32).reshape(DECODE_ROWS, DECODE_STEPS, QUERY_HEADS, HEAD_SIZE)
    key_value_unshaped = jnp.dot(flat_layout, fresh_weights.reshape(MODEL_WIDTH, 2 * KEY_FEATURES), preferred_element_type=jnp.float32).reshape(DECODE_ROWS, DECODE_STEPS, 2, KEY_VALUE_HEADS, HEAD_SIZE)
    positions = lengths[:, None] + jnp.arange(DECODE_STEPS, dtype=jnp.int32)[None, :]
    query_vectors = rotate(head_norm(qraw), positions).astype(jnp.bfloat16)
    new_keys = rotate(head_norm(key_value_unshaped[:, :, 0]), positions).astype(jnp.bfloat16)
    new_values = key_value_unshaped[:, :, 1].astype(jnp.bfloat16)
    new_kv = jnp.stack([new_keys, new_values]).transpose(0, 1, 3, 2, 4)
    grouped_query = query_vectors.reshape(DECODE_ROWS, DECODE_STEPS, KEY_VALUE_HEADS, QUERY_HEADS // KEY_VALUE_HEADS, HEAD_SIZE)

    def one_row(items):
        q_row, k_old, v_old, k_new, v_new, length = items
        return attend_row(q_row, k_old, v_old, k_new, v_new, length)
    attended = lax.map(one_row, (grouped_query, cache[0], cache[1], new_keys, new_values, lengths))
    attended = attended.reshape(DECODE_ROWS, DECODE_STEPS, QD)
    return (new_weight, new_moment, new_second, new_kv, attended)
```

```python
import functools
import math

import jax
import jax.numpy as jnp
from jax import lax
from jax.experimental import pallas as pl
from jax.experimental.pallas import tpu as pltpu
from jax.sharding import PartitionSpec as P

MESH = pl.DeviceIdType.MESH
BF16 = jnp.bfloat16
F32 = jnp.float32

WIDTH = 5120
TOK = 1024
HEAD = 128
HEADS = 8
STEPS = 3
VOCAB_OWN = 4864
POSITIONS = 4096
OWN = 320
CHUNK = 640
PAD = 8

learn_rate = 0.002
beta_one = 0.9
beta_two = 0.95
bias_one = 1.0 - 0.9**10
bias_two = 1.0 - 0.95**10
adam_eps = 1e-08
weight_decay = 0.1
norm_eps = 1e-06
rope_log = math.log(1000000.0)


def adam(weight, moment, second, grad):
    new_moment = beta_one * moment + (1.0 - beta_one) * grad
    new_second = beta_two * second + (1.0 - beta_two) * grad * grad
    update = new_moment / bias_one / (jnp.sqrt(new_second / bias_two) + adam_eps)
    new_weight = weight - learn_rate * (update + weight_decay * weight)
    return new_weight, new_moment, new_second


def head_norm(values):
    return values * lax.rsqrt(jnp.mean(values * values, axis=-1, keepdims=True) + norm_eps)


def kernel(
    li_hbm,
    cot_hbm,
    w_hbm,
    m_hbm,
    v_hbm,
    table_hbm,
    gain_ref,
    qw_hbm,
    cache_hbm,
    ids_ref,
    cos_ref,
    sin_ref,
    len_ref,
    grad_ref,
    kv_ref,
    att_ref,
    li,
    cot,
    cotf,
    cot_t,
    wm,
    table,
    qw,
    cache,
    core_send,
    core_recv,
    own,
    part,
    recv1,
    send2,
    recv2,
    send3,
    recv3,
    e1_pick,
    e1a_recv,
    e1_sum,
    e1b_recv,
    e2,
    tiles,
    normed,
    qraw,
    e3_send,
    e3_recv,
    fresh,
    kv_send,
    kv_recv,
    load_sem,
    core_sem,
    s1_sem,
    s2_sem,
    s3_sem,
    e1a_sem,
    e1b_sem,
    e2_sem,
    e3_sem,
    kv_sem,
):
    c, f, t = lax.axis_index("group"), lax.axis_index("fsdp"), lax.axis_index("tp")
    x, h = f // 2, f % 2
    gf = c * 8 + f
    other_c = 1 - c
    near_a = x + 1 - 2 * (x % 2)
    near_b = 3 - x
    far = (x + 2) % 4
    order = (far, near_a, near_b, x)

    core_peer = (other_c, f, t)
    a_peer = (c, near_a * 2 + h, t)
    b_peer = (c, near_b * 2 + h, t)
    h_peer = (c, x * 2 + 1 - h, t)

    def gf_peer(d):
        there = (gf + d) % 16
        return (there // 8, there % 8, t)

    def f_peer(d):
        return (c, (f + d) % 8, t)

    def tp_peer(d):
        return (c, f, (t + d) % 8)

    def remote(src, dst, sems, index, peer):
        return pltpu.make_async_remote_copy(
            src_ref=src,
            dst_ref=dst,
            send_sem=sems.at[(0,) + index],
            recv_sem=sems.at[(1,) + index],
            device_id=peer,
            device_id_type=MESH,
        )

    def load(src, dst, n):
        return pltpu.make_async_copy(src, dst, load_sem.at[n])

    def li_load(j):
        core = other_c if j % 2 == 0 else c
        column = pl.multiple_of(core * 2560 + order[j // 2] * CHUNK, 128)
        return load(li_hbm.at[:, pl.ds(column, CHUNK)], li.at[j], j)

    cot_load = load(cot_hbm, cot, 8)
    table_load = load(table_hbm, table, 9)
    w_loads = [load(ref, wm.at[n], 10 + n) for n, ref in enumerate((w_hbm, m_hbm, v_hbm))]
    qw_load = load(qw_hbm, qw, 13)
    cache_load = load(cache_hbm, cache, 14)

    cot_load.start()
    li_load(0).start()
    li_load(1).start()
    table_load.start()
    for j in range(2, 8):
        li_load(j).start()

    barrier = pltpu.get_barrier_semaphore()
    for d in range(1, 16):
        pl.semaphore_signal(barrier, inc=1, device_id=gf_peer(d), device_id_type=MESH)
    for d in range(1, 8):
        pl.semaphore_signal(barrier, inc=1, device_id=tp_peer(d), device_id_type=MESH)

    cot_load.wait()
    cotf[...] = cot[...].astype(F32)
    for n in range(2):
        cot_t[pl.ds(n * HEAD, HEAD), :] = cotf[pl.ds(n, TOK, 2), :].T.astype(BF16)

    def term(j):
        li_load(j).wait()
        return jnp.dot(cot_t[...], li[j], preferred_element_type=F32).T

    def core_copy(i):
        return remote(core_send.at[i], core_recv.at[i], core_sem, (i,), core_peer)

    def terms(i):
        core_send[i] = term(2 * i).astype(BF16)
        if i == 0:
            pl.semaphore_wait(barrier, 22)
        core_copy(i).start()
        own[i] = term(2 * i + 1)

    def add_cores(i):
        core_copy(i).wait_recv()
        for ab in range(2):
            lanes = pl.ds(ab * HEAD, HEAD)
            part[i, ab] = (own[i, :, lanes] + core_recv[i, :, lanes].astype(F32)).astype(BF16)

    def half(way):
        return pl.ds(pl.multiple_of((1 - h if way == 0 else h) * OWN, 64), OWN)

    peers = (a_peer, b_peer)

    def step1(i, ab, slot, way):
        return remote(
            part.at[i, ab, half(way)], recv1.at[ab, slot, way], s1_sem, (ab, slot, way), peers[ab]
        )

    def step2(ab, way):
        return remote(
            send2.at[ab, way], recv2.at[ab, way], s2_sem, (ab, way), peers[1 - ab]
        )

    def step2_go(way):
        for ab, i in ((0, 2), (1, 1)):
            step1(i, ab, 0, way).wait_recv()
            send2[ab, way] = (
                part[i, ab, half(way)].astype(F32) + recv1[ab, 0, way].astype(F32)
            ).astype(BF16)
            step2(ab, way).start()

    def step3(ab):
        return remote(send3.at[ab], recv3.at[ab], s3_sem, (ab,), h_peer)

    def x_sum(ab, way):
        step1(3, ab, 1, way).wait_recv()
        step2(ab, way).wait_recv()
        return (
            part[3, ab, half(way)].astype(F32)
            + recv1[ab, 1, way].astype(F32)
            + recv2[ab, way].astype(F32)
        )

    terms(0)

    table_load.wait()
    local = ids_ref[...] - gf * VOCAB_OWN
    hot = jnp.where(
        lax.broadcasted_iota(jnp.int32, (16 * PAD, VOCAB_OWN), 1) == local, 1.0, 0.0
    ).astype(BF16)
    picked = jnp.dot(hot, table[...], preferred_element_type=F32)
    blank = jnp.zeros((PAD, HEAD), F32)
    for device in range(16):
        rows = picked[device * PAD : (device + 1) * PAD]
        e1_pick[device // 8, device % 8] = jnp.concatenate(
            [rows[:, b * HEAD : (b + 1) * HEAD] for b in range(5)] + [blank], axis=0
        ).astype(BF16)
    e1a = remote(e1_pick.at[other_c], e1a_recv, e1a_sem, (), core_peer)
    e1a.start()

    terms(1)
    add_cores(0)
    for way in range(2):
        step1(0, 0, 0, way).start()
        step1(0, 1, 0, way).start()

    e1a.wait_recv()
    e1_sum[...] = (e1_pick[c].astype(F32) + e1a_recv[...].astype(F32)).astype(BF16)

    def e1b(d):
        return remote(e1_sum.at[(f + d) % 8], e1b_recv.at[d], e1b_sem, (d,), f_peer(d))

    for d in range(1, 8):
        e1b(d).start()

    qw_load.start()
    terms(2)
    add_cores(1)
    for way in range(2):
        step1(1, 0, 1, way).start()
    cache_load.start()
    terms(3)
    add_cores(2)
    for way in range(2):
        step1(2, 1, 1, way).start()
    for one in w_loads:
        one.start()

    mine = e1_sum[f].astype(F32)
    for d in range(1, 8):
        e1b(d).wait_recv()
        mine = mine + e1b_recv[d].astype(F32)
    e2[t] = mine.astype(BF16)

    def e2_copy(d):
        return remote(e2.at[t], e2.at[t], e2_sem, (d,), tp_peer(d))

    def e2_arrival(d):
        there = (t + 8 - d) % 8
        return remote(e2.at[there], e2.at[there], e2_sem, (d,), tp_peer(d))

    for d in range(1, 8):
        e2_copy(d).start()

    add_cores(3)
    step2_go(0)

    for d in range(1, 8):
        e2_arrival(d).wait_recv()
    square = jnp.zeros((PAD, HEAD), F32)
    for n in range(8):
        emb = e2[n].astype(F32)
        for b in range(5):
            one = emb[b * PAD : (b + 1) * PAD]
            square = square + one * one
    mean = jnp.sum(square, axis=-1, keepdims=True) * (1.0 / WIDTH)
    factor = lax.rsqrt(mean + norm_eps)
    for n in range(8):
        emb = e2[n].astype(F32)
        for b in range(5):
            k = n * 5 + b
            one = emb[b * PAD : (b + 1) * PAD] * gain_ref[:, pl.ds(k * HEAD, HEAD)] * factor
            one = one.astype(BF16).astype(F32)
            tiles[pl.ds(k * PAD, PAD), :] = one
            normed[:, pl.ds(k * HEAD, HEAD)] = one
    tiles[pl.ds(40 * PAD, 2 * PAD), :] = jnp.zeros((2 * PAD, HEAD), F32)

    def e3_block(device):
        first = (device // 2) * 5 + 2 * (device % 2)
        return tiles[pl.ds(pl.multiple_of(first * PAD, PAD), 4 * PAD), :].astype(BF16)

    def e3(d):
        return remote(e3_send.at[d], e3_recv.at[d], e3_sem, (d,), gf_peer(d))

    for d in range(1, 16):
        e3_send[d] = e3_block((gf + d) % 16)
        e3(d).start()
    e3_recv[0] = e3_block(gf)

    step2_go(1)

    qw_load.wait()
    normed16 = normed[...].astype(BF16)

    @pl.loop(0, 4)
    def _(n):
        columns = pl.ds(pl.multiple_of(n * 256, 256), 256)
        qraw[:, columns] = jnp.dot(normed16, qw[:, columns], preferred_element_type=F32)

    cosine, sine = cos_ref[...], sin_ref[...]

    def rotate(values):
        return values * cosine + pltpu.roll(values, HEAD // 2, 1) * sine

    query = jnp.concatenate(
        [rotate(head_norm(qraw[:, g * HEAD : (g + 1) * HEAD])) for g in range(HEADS)], axis=0
    ).astype(BF16)

    for ab in range(2):
        send3[ab] = x_sum(ab, 0).astype(BF16)
        step3(ab).start()

    scale = 1.0 / math.sqrt(HEAD)
    cache_load.wait()
    block = 1024
    sums = []
    for r in range(2):
        length = len_ref[r]

        def attend(n, carry, r=r, length=length):
            denom, numer = carry
            where = pl.ds(pl.multiple_of(n * block, block), block)
            scores = lax.dot_general(
                query, cache[0, r, where, :], (((1,), (1,)), ((), ())), preferred_element_type=F32
            )
            position = lax.broadcasted_iota(jnp.int32, scores.shape, 1) + n * block
            weights = jnp.where(position < length, jnp.exp(scores * scale), 0.0)
            denom = denom + jnp.sum(weights, axis=-1, keepdims=True)
            numer = numer + jnp.dot(
                weights.astype(BF16), cache[1, r, where, :], preferred_element_type=F32
            )
            return denom, numer

        rows = HEADS * PAD
        sums.append(
            lax.fori_loop(
                0,
                POSITIONS // block,
                attend,
                (jnp.zeros((rows, 1), F32), jnp.zeros((rows, HEAD), F32)),
            )
        )
    token = lax.broadcasted_iota(jnp.int32, (HEADS * PAD, 1), 0) % PAD
    first_row = token < STEPS
    denom = jnp.where(first_row, sums[0][0], sums[1][0])
    numer = jnp.where(first_row, sums[0][1], sums[1][1])

    for d in range(1, 16):
        e3(d).wait_recv()
    arrived = [e3_recv[d].astype(F32) for d in range(16)]
    features = jnp.concatenate(
        [
            jnp.concatenate([one[b * PAD : (b + 1) * PAD] for one in arrived], axis=0)
            for b in range(3)
        ],
        axis=1,
    ).astype(BF16)

    fresh[...] = jnp.zeros_like(fresh)
    for one in w_loads:
        one.wait()
    for ab in range(2):
        total = x_sum(ab, 1)
        step3(ab).wait_recv()
        total = total + recv3[ab].astype(F32)
        every = pl.ds(ab, OWN, 2)
        grad_ref[every, :] = total
        new_weight, _, _ = adam(wm[0, every, :], wm[1, every, :], wm[2, every, :], total)
        fresh[pl.ds(pl.multiple_of(h * 64, 64), OWN), pl.ds(ab * HEAD, HEAD)] = new_weight.astype(
            BF16
        )
    partial = jnp.dot(features, fresh[...], preferred_element_type=F32)

    def kv(d):
        return remote(kv_send.at[d], kv_recv.at[d], kv_sem, (d,), gf_peer(16 - d))

    for d in range(1, 16):
        rows = partial[d * PAD : (d + 1) * PAD]
        kv_send[d] = jnp.concatenate([rows[:, :HEAD], rows[:, HEAD:]], axis=0).astype(BF16)
        kv(d).start()
    total = jnp.concatenate([partial[:PAD, :HEAD], partial[:PAD, HEAD:]], axis=0)
    for d in range(1, 16):
        kv(d).wait_recv()
        total = total + kv_recv[d].astype(F32)
    new_key = rotate(head_norm(total[:PAD])).astype(BF16).astype(F32)
    new_value = total[PAD:].astype(BF16).astype(F32)
    kv_ref[0] = new_key
    kv_ref[1] = new_value

    query32 = query.astype(F32)
    for j in range(2 * STEPS):
        score = jnp.sum(query32 * new_key[j : j + 1], axis=-1, keepdims=True) * scale
        seen = (token // STEPS == j // STEPS) & (token >= j)
        weight = jnp.where(seen, jnp.exp(score), 0.0)
        denom = denom + weight
        numer = numer + weight.astype(BF16).astype(F32) * new_value[j : j + 1]
    attended = numer / denom
    for g in range(HEADS):
        att_ref[:, pl.ds(g * HEAD, HEAD)] = attended[g * PAD : (g + 1) * PAD]

    for i in range(4):
        core_copy(i).wait_send()
    for way in range(2):
        for ab in range(2):
            step1(0, ab, 0, way).wait_send()
            step1(1 + ab, ab, 1, way).wait_send()
            step2(ab, way).wait_send()
    for ab in range(2):
        step3(ab).wait_send()
    e1a.wait_send()
    for d in range(1, 8):
        e1b(d).wait_send()
        e2_copy(d).wait_send()
    for d in range(1, 16):
        e3(d).wait_send()
        kv(d).wait_send()


def shards(
    learn_input,
    learn_cotangent,
    weight,
    moment,
    second,
    table,
    gain,
    query_weight,
    cache,
    token_ids,
    lengths,
):
    rows = lengths.shape[0]
    tokens = rows * STEPS

    ids = jnp.pad(token_ids.reshape(16, tokens), ((0, 0), (0, PAD - tokens)), constant_values=-1)
    ids = ids.reshape(16 * PAD, 1)
    positions = (lengths[:, None] + jnp.arange(STEPS, dtype=jnp.int32)[None, :]).reshape(tokens, 1)
    half = HEAD // 2
    freqs = jnp.exp(-rope_log * 2.0 * jnp.arange(half, dtype=F32) / HEAD)
    angles = positions.astype(F32) * freqs
    angles = jnp.pad(angles, ((0, PAD - tokens), (0, 0)))
    cosine, sine = jnp.cos(angles), jnp.sin(angles)
    cosine = jnp.concatenate([cosine, cosine], axis=1)
    sine = jnp.concatenate([-sine, sine], axis=1)

    anywhere = pl.BlockSpec(memory_space=pl.ANY)
    vmem = pl.BlockSpec(memory_space=pltpu.VMEM)
    smem = pl.BlockSpec(memory_space=pltpu.SMEM)
    dma = pltpu.SemaphoreType.DMA
    grad, kv, att = pl.pallas_call(
        kernel,
        out_shape=(
            jax.ShapeDtypeStruct((2 * OWN, HEAD), F32),
            jax.ShapeDtypeStruct((2, PAD, HEAD), F32),
            jax.ShapeDtypeStruct((PAD, HEADS * HEAD), F32),
        ),
        in_specs=[anywhere] * 6 + [vmem] + [anywhere] * 2 + [vmem] * 3 + [smem],
        out_specs=(vmem, vmem, vmem),
        scratch_shapes=[
            pltpu.VMEM((8, TOK, CHUNK), BF16),
            pltpu.VMEM((2 * TOK, HEAD), BF16),
            pltpu.VMEM((2 * TOK, HEAD), F32),
            pltpu.VMEM((2 * HEAD, TOK), BF16),
            pltpu.VMEM((3, 2 * OWN, HEAD), F32),
            pltpu.VMEM((VOCAB_OWN, CHUNK), BF16),
            pltpu.VMEM((WIDTH, HEADS * HEAD), BF16),
            pltpu.VMEM((2, 2, POSITIONS, HEAD), BF16),
            pltpu.VMEM((4, CHUNK, 2 * HEAD), BF16),
            pltpu.VMEM((4, CHUNK, 2 * HEAD), BF16),
            pltpu.VMEM((4, CHUNK, 2 * HEAD), F32),
            pltpu.VMEM((4, 2, CHUNK, HEAD), BF16),
            pltpu.VMEM((2, 2, 2, OWN, HEAD), BF16),
            pltpu.VMEM((2, 2, OWN, HEAD), BF16),
            pltpu.VMEM((2, 2, OWN, HEAD), BF16),
            pltpu.VMEM((2, OWN, HEAD), BF16),
            pltpu.VMEM((2, OWN, HEAD), BF16),
            pltpu.VMEM((2, 8, 6 * PAD, HEAD), BF16),
            pltpu.VMEM((8, 6 * PAD, HEAD), BF16),
            pltpu.VMEM((8, 6 * PAD, HEAD), BF16),
            pltpu.VMEM((8, 6 * PAD, HEAD), BF16),
            pltpu.VMEM((8, 6 * PAD, HEAD), BF16),
            pltpu.VMEM((42 * PAD, HEAD), F32),
            pltpu.VMEM((PAD, WIDTH), F32),
            pltpu.VMEM((PAD, HEADS * HEAD), F32),
            pltpu.VMEM((16, 4 * PAD, HEAD), BF16),
            pltpu.VMEM((16, 4 * PAD, HEAD), BF16),
            pltpu.VMEM((3 * HEAD, 2 * HEAD), BF16),
            pltpu.VMEM((16, 2 * PAD, HEAD), BF16),
            pltpu.VMEM((16, 2 * PAD, HEAD), BF16),
            dma((15,)),
            dma((2, 4)),
            dma((2, 2, 2, 2)),
            dma((2, 2, 2)),
            dma((2, 2)),
            dma((2,)),
            dma((2, 8)),
            dma((2, 8)),
            dma((2, 16)),
            dma((2, 16)),
        ],
        compiler_params=pltpu.CompilerParams(
            collective_id=0, has_side_effects=True, vmem_limit_bytes=60 * 1024 * 1024
        ),
        name="step",
    )(
        learn_input,
        learn_cotangent.reshape(2 * TOK, HEAD),
        weight.reshape(2 * OWN, HEAD),
        moment.reshape(2 * OWN, HEAD),
        second.reshape(2 * OWN, HEAD),
        table,
        gain.astype(F32).reshape(1, WIDTH),
        query_weight,
        cache.reshape(2, rows, POSITIONS, HEAD),
        ids,
        cosine,
        sine,
        lengths,
    )
    new_weight, new_moment, new_second = adam(
        weight, moment, second, grad.reshape(OWN, 2, HEAD)
    )
    new_kv = kv[:, :tokens].reshape(2, rows, 1, STEPS, HEAD).astype(BF16)
    attended = att[:tokens].reshape(rows, STEPS, HEADS * HEAD).astype(BF16)
    return new_weight, new_moment, new_second, new_kv, attended


def solution(mesh):
    return jax.shard_map(
        shards,
        mesh=mesh,
        in_specs=(
            P(("group", "fsdp"), None),
            P(("group", "fsdp"), None, "tp"),
            P(("group", "fsdp"), None, "tp"),
            P(("group", "fsdp"), None, "tp"),
            P(("group", "fsdp"), None, "tp"),
            P(("group", "fsdp"), "tp"),
            P(),
            P(None, "tp"),
            P(None, ("group", "fsdp"), "tp", None, None),
            P(),
            P(("group", "fsdp")),
        ),
        out_specs=(
            P(("group", "fsdp"), None, "tp"),
            P(("group", "fsdp"), None, "tp"),
            P(("group", "fsdp"), None, "tp"),
            P(None, ("group", "fsdp"), "tp", None, None),
            P(("group", "fsdp"), None, "tp"),
        ),
        check_vma=False,
    )
```

```python
import functools
import math

import jax
import jax.numpy as jnp
from jax import lax
from jax.experimental import pallas as pl
from jax.experimental.pallas import tpu as pltpu
from jax.sharding import PartitionSpec as P

MESH = pl.DeviceIdType.MESH
BF16 = jnp.bfloat16
F32 = jnp.float32

WIDTH = 5120
TOK = 1024
HEAD = 128
HEADS = 8
STEPS = 3
VOCAB_OWN = 4864
POSITIONS = 4096
OWN = 320
CHUNK = 640
PAD = 8

learn_rate = 0.002
beta_one = 0.9
beta_two = 0.95
bias_one = 1.0 - 0.9**10
bias_two = 1.0 - 0.95**10
adam_eps = 1e-08
weight_decay = 0.1
norm_eps = 1e-06
rope_log = math.log(1000000.0)


def adam(weight, moment, second, grad):
    new_moment = beta_one * moment + (1.0 - beta_one) * grad
    new_second = beta_two * second + (1.0 - beta_two) * grad * grad
    update = new_moment / bias_one / (jnp.sqrt(new_second / bias_two) + adam_eps)
    new_weight = weight - learn_rate * (update + weight_decay * weight)
    return new_weight, new_moment, new_second


def head_norm(values):
    return values * lax.rsqrt(jnp.mean(values * values, axis=-1, keepdims=True) + norm_eps)


def kernel(
    li_hbm,
    cot_hbm,
    w_hbm,
    m_hbm,
    v_hbm,
    table_hbm,
    gain_hbm,
    qw_hbm,
    cache_hbm,
    ids_hbm,
    len_hbm,
    grad_hbm,
    kv_ref,
    att_ref,
    li,
    cot,
    cotf,
    cot_t,
    wm,
    table,
    qw,
    cache,
    core_send,
    core_recv,
    own,
    part,
    recv1,
    send2,
    recv2,
    send3,
    recv3,
    e1_send,
    e1_recv,
    e2,
    scaled,
    qraw,
    e3_recv,
    fresh,
    kv_send,
    kv_recv,
    gain,
    gain32,
    ids,
    len_ref,
    grad,
    load_sem,
    core_sem,
    s1_sem,
    s2_sem,
    s3_sem,
    e1_sem,
    e2_sem,
    e3_sem,
    kv_sem,
):
    c, f, t = lax.axis_index("group"), lax.axis_index("fsdp"), lax.axis_index("tp")
    x, h = f // 2, f % 2
    gf = c * 8 + f
    other_c = 1 - c
    near_a = x + 1 - 2 * (x % 2)
    near_b = 3 - x
    far = (x + 2) % 4
    order = (far, near_a, near_b, x)

    core_peer = (other_c, f, t)
    a_peer = (c, near_a * 2 + h, t)
    b_peer = (c, near_b * 2 + h, t)
    h_peer = (c, x * 2 + 1 - h, t)

    def gf_peer(d):
        there = (gf + d) % 16
        return (there // 8, there % 8, t)

    def tp_peer(d):
        return (c, f, (t + d) % 8)

    def remote(src, dst, sems, index, peer):
        return pltpu.make_async_remote_copy(
            src_ref=src,
            dst_ref=dst,
            send_sem=sems.at[(0,) + index],
            recv_sem=sems.at[(1,) + index],
            device_id=peer,
            device_id_type=MESH,
        )

    def load(src, dst, n):
        return pltpu.make_async_copy(src, dst, load_sem.at[n])

    def li_load(j):
        core = other_c if j % 2 == 0 else c
        column = pl.multiple_of(core * 2560 + order[j // 2] * CHUNK, 128)
        return load(li_hbm.at[:, pl.ds(column, CHUNK)], li.at[j], j)

    cot_load = load(cot_hbm, cot, 8)
    table_load = load(table_hbm, table, 9)
    w_loads = [load(ref, wm.at[n], 10 + n) for n, ref in enumerate((w_hbm, m_hbm, v_hbm))]
    qw_load = load(qw_hbm, qw, 13)
    cache_load = load(cache_hbm, cache, 14)

    small_loads = [load(ids_hbm, ids, 15), load(len_hbm, len_ref, 16), load(gain_hbm, gain, 17)]

    cot_load.start()
    for one in small_loads:
        one.start()
    table_load.start()
    for j in range(8):
        li_load(j).start()

    barrier = pltpu.get_barrier_semaphore()
    for d in range(1, 16):
        pl.semaphore_signal(barrier, inc=1, device_id=gf_peer(d), device_id_type=MESH)
    for d in range(1, 8):
        pl.semaphore_signal(barrier, inc=1, device_id=tp_peer(d), device_id_type=MESH)

    cot_load.wait()
    cotf[...] = cot[...].astype(F32)
    for n in range(2):
        cot_t[pl.ds(n * HEAD, HEAD), :] = cotf[pl.ds(n, TOK, 2), :].T.astype(BF16)

    def term(j):
        li_load(j).wait()
        return jnp.dot(cot_t[...], li[j], preferred_element_type=F32).T

    def core_copy(i):
        return remote(core_send.at[i], core_recv.at[i], core_sem, (i,), core_peer)

    def terms(i):
        core_send[i] = term(2 * i).astype(BF16)
        if i == 0:
            pl.semaphore_wait(barrier, 22)
        core_copy(i).start()
        if i == 0:
            for d in range(1, 16):
                e1(d).start()
        own[i] = term(2 * i + 1)

    def add_cores(i):
        core_copy(i).wait_recv()
        for ab in range(2):
            lanes = pl.ds(ab * HEAD, HEAD)
            part[i, ab] = (own[i, :, lanes] + core_recv[i, :, lanes].astype(F32)).astype(BF16)

    def half(way):
        return pl.ds(pl.multiple_of((1 - h if way == 0 else h) * OWN, 64), OWN)

    peers = (a_peer, b_peer)

    def step1(i, ab, slot, way):
        return remote(
            part.at[i, ab, half(way)], recv1.at[ab, slot, way], s1_sem, (ab, slot, way), peers[ab]
        )

    def step2(ab, way):
        return remote(
            send2.at[ab, way], recv2.at[ab, way], s2_sem, (ab, way), peers[1 - ab]
        )

    def step2_go(way):
        for ab, i in ((0, 2), (1, 1)):
            step1(i, ab, 0, way).wait_recv()
            send2[ab, way] = (
                part[i, ab, half(way)].astype(F32) + recv1[ab, 0, way].astype(F32)
            ).astype(BF16)
            step2(ab, way).start()

    def step3(ab):
        return remote(send3.at[ab], recv3.at[ab], s3_sem, (ab,), h_peer)

    def x_sum(ab, way):
        step1(3, ab, 1, way).wait_recv()
        step2(ab, way).wait_recv()
        return (
            part[3, ab, half(way)].astype(F32)
            + recv1[ab, 1, way].astype(F32)
            + recv2[ab, way].astype(F32)
        )

    for one in small_loads:
        one.wait()
    slot = lax.broadcasted_iota(jnp.int32, (16 * PAD, 32), 0)
    row = lax.broadcasted_iota(jnp.int32, (16 * PAD, 32), 1)
    place = slot % PAD
    mine = row == 2 * (slot // PAD) + place % 2
    wanted = jnp.zeros((16 * PAD, 32), F32)
    for step in range(STEPS):
        here = mine & (place // 2 == step)
        wanted = wanted + jnp.where(here, ids[step : step + 1, :].astype(F32), 0.0)
    wanted = jnp.sum(wanted, axis=-1, keepdims=True).astype(jnp.int32)
    wanted = jnp.where(place[:, :1] < 2 * STEPS, wanted, -1)
    hot = jnp.where(
        lax.broadcasted_iota(jnp.int32, (16 * PAD, VOCAB_OWN), 1) == wanted - gf * VOCAB_OWN, 1.0, 0.0
    ).astype(BF16)
    table_load.wait()
    picked = jnp.dot(hot, table[...], preferred_element_type=F32)
    blank = jnp.zeros((PAD, HEAD), F32)
    for device in range(16):
        rows = picked[device * PAD : (device + 1) * PAD]
        e1_send[device] = jnp.concatenate(
            [rows[:, b * HEAD : (b + 1) * HEAD] for b in range(5)] + [blank], axis=0
        ).astype(BF16)

    def e1(d):
        return remote(e1_send.at[(gf + d) % 16], e1_recv.at[d], e1_sem, (d,), gf_peer(d))

    terms(0)
    qw_load.start()
    terms(1)
    add_cores(0)
    step1(0, 0, 0, 0).start()
    step1(0, 1, 0, 0).start()
    cache_load.start()
    for one in w_loads:
        one.start()
    terms(2)
    add_cores(1)
    step1(1, 0, 1, 0).start()
    terms(3)
    add_cores(2)
    step1(2, 1, 1, 0).start()
    add_cores(3)
    step2_go(0)
    step1(0, 0, 0, 1).start()
    step1(0, 1, 0, 1).start()
    step1(1, 0, 1, 1).start()
    step1(2, 1, 1, 1).start()

    total = e1_send[gf].astype(F32)
    for d in range(1, 16):
        e1(d).wait_recv()
        total = total + e1_recv[d].astype(F32)
    e2[t] = total.astype(BF16)

    lined = gf // 2 == t

    def e3(a, b):
        to_h, to_t = (h + a) % 2, (t + b) % 8
        return pltpu.make_async_remote_copy(
            src_ref=e2.at[t, pl.ds(pl.multiple_of(16 * to_h, 16), 4 * PAD)],
            dst_ref=e3_recv.at[gf],
            send_sem=e3_sem.at[0, 8 * a + b],
            recv_sem=e3_sem.at[1, gf],
            device_id=(t // 4, (t % 4) * 2 + to_h, to_t),
            device_id_type=MESH,
        )

    def e3_arrival(d):
        source = (gf + d) % 16
        return pltpu.make_async_remote_copy(
            src_ref=e2.at[t, pl.ds(0, 4 * PAD)],
            dst_ref=e3_recv.at[source],
            send_sem=e3_sem.at[0, 0],
            recv_sem=e3_sem.at[1, source],
            device_id=gf_peer(1),
            device_id_type=MESH,
        )

    for a in range(2):
        for b in range(8):
            if a + b:
                e3(a, b).start()

    @pl.when(jnp.logical_not(lined))
    def _():
        e3(0, 0).start()

    @pl.when(lined)
    def _():
        e3_recv[gf] = e2[t, pl.ds(pl.multiple_of(16 * h, 16), 4 * PAD), :]

    def e2_copy(d):
        return remote(e2.at[t], e2.at[t], e2_sem, (d,), tp_peer(d))

    def e2_arrival(d):
        there = (t + 8 - d) % 8
        return remote(e2.at[there], e2.at[there], e2_sem, (d,), tp_peer(d))

    for d in range(1, 8):
        e2_copy(d).start()

    gain32[...] = gain[...].astype(F32)
    fresh[...] = jnp.zeros_like(fresh)

    for ab in range(2):
        send3[ab] = x_sum(ab, 0).astype(BF16)
        step3(ab).start()

    step2_go(1)

    for d in range(1, 8):
        e2_arrival(d).wait_recv()
    square = jnp.zeros((PAD, HEAD), F32)
    for n in range(8):
        emb = e2[n].astype(F32)
        for b in range(5):
            k = n * 5 + b
            one = emb[b * PAD : (b + 1) * PAD]
            square = square + one * one
            scaled[:, k * HEAD : (k + 1) * HEAD] = one * gain32[k : k + 1, :]
    mean = jnp.sum(square, axis=-1, keepdims=True) * (1.0 / WIDTH)
    factor = lax.rsqrt(mean + norm_eps)

    qw_load.wait()
    scaled16 = scaled[...].astype(BF16)

    @pl.loop(0, 4)
    def _(n):
        columns = pl.ds(pl.multiple_of(n * 256, 256), 256)
        qraw[:, columns] = jnp.dot(scaled16, qw[:, columns], preferred_element_type=F32)

    place = lax.broadcasted_iota(jnp.int32, (PAD, HEAD), 0)
    lane = lax.broadcasted_iota(jnp.int32, (PAD, HEAD), 1)
    position = jnp.where(place % 2 == 0, len_ref[0], len_ref[1]) + place // 2
    freqs = jnp.exp((lane % (HEAD // 2)).astype(F32) * (-rope_log * 2.0 / HEAD))
    angles = position.astype(F32) * freqs
    cosine, sine = jnp.cos(angles), jnp.sin(angles)
    sine = jnp.where(lane < HEAD // 2, -sine, sine)

    def rotate(values):
        return values * cosine + pltpu.roll(values, HEAD // 2, 1) * sine

    query = jnp.concatenate(
        [
            rotate(head_norm(qraw[:, g * HEAD : (g + 1) * HEAD] * factor))
            for g in range(HEADS)
        ],
        axis=0,
    ).astype(BF16)

    @pl.when(jnp.logical_not(lined))
    def _():
        e3_arrival(0).wait_recv()

    for d in range(1, 16):
        e3_arrival(d).wait_recv()
    first = (gf // 2) * 5 + 2 * h
    arrived = [e3_recv[n].astype(F32) for n in range(16)]
    features = jnp.concatenate(
        [
            jnp.concatenate([one[b * PAD : (b + 1) * PAD] for one in arrived], axis=0)
            * gain32[pl.ds(first + b, 1), :]
            for b in range(3)
        ],
        axis=1,
    ).astype(BF16)

    for one in w_loads:
        one.wait()
    for ab in range(2):
        total = x_sum(ab, 1)
        step3(ab).wait_recv()
        total = total + recv3[ab].astype(F32)
        every = pl.ds(ab, OWN, 2)
        grad[every, :] = total
        new_weight, _, _ = adam(wm[0, every, :], wm[1, every, :], wm[2, every, :], total)
        fresh[pl.ds(pl.multiple_of(h * 64, 64), OWN), pl.ds(ab * HEAD, HEAD)] = new_weight.astype(
            BF16
        )
    partial = jnp.dot(features, fresh[...], preferred_element_type=F32)

    def kv(d):
        return remote(kv_send.at[(gf + d) % 16], kv_recv.at[d], kv_sem, (d,), gf_peer(d))

    for n in range(16):
        rows = partial[n * PAD : (n + 1) * PAD]
        kv_send[n] = jnp.concatenate([rows[:, :HEAD], rows[:, HEAD:]], axis=0).astype(BF16)
    for d in range(1, 16):
        kv(d).start()
    grad_store = load(grad, grad_hbm, 18)
    grad_store.start()

    scale = 1.0 / math.sqrt(HEAD)
    cache_load.wait()
    block = 1024
    sums = []
    for r in range(2):
        length = len_ref[r]

        def attend(n, carry, r=r, length=length):
            denom, numer = carry
            where = pl.ds(pl.multiple_of(n * block, block), block)
            scores = lax.dot_general(
                query, cache[0, r, where, :], (((1,), (1,)), ((), ())), preferred_element_type=F32
            )
            position = lax.broadcasted_iota(jnp.int32, scores.shape, 1) + n * block
            weights = jnp.where(position < length, jnp.exp(scores * scale), 0.0)
            denom = denom + jnp.sum(weights, axis=-1, keepdims=True)
            numer = numer + jnp.dot(
                weights.astype(BF16), cache[1, r, where, :], preferred_element_type=F32
            )
            return denom, numer

        rows = HEADS * PAD
        sums.append(
            lax.fori_loop(
                0,
                POSITIONS // block,
                attend,
                (jnp.zeros((rows, 1), F32), jnp.zeros((rows, HEAD), F32)),
            )
        )
    token = lax.broadcasted_iota(jnp.int32, (HEADS * PAD, 1), 0) % PAD
    first_row = token % 2 == 0
    denom = jnp.where(first_row, sums[0][0], sums[1][0])
    numer = jnp.where(first_row, sums[0][1], sums[1][1])

    total = kv_send[gf].astype(F32)
    for d in range(1, 16):
        kv(d).wait_recv()
        total = total + kv_recv[d].astype(F32)
    new_key = rotate(head_norm(total[:PAD] * factor)).astype(BF16).astype(F32)
    new_value = (total[PAD:] * factor).astype(BF16).astype(F32)
    kv_ref[0] = new_key
    kv_ref[1] = new_value

    query32 = query.astype(F32)
    for j in range(2 * STEPS):
        score = jnp.sum(query32 * new_key[j : j + 1], axis=-1, keepdims=True) * scale
        seen = (token % 2 == j % 2) & (token >= j)
        weight = jnp.where(seen, jnp.exp(score), 0.0)
        denom = denom + weight
        numer = numer + weight.astype(BF16).astype(F32) * new_value[j : j + 1]
    attended = numer / denom
    for g in range(HEADS):
        att_ref[:, pl.ds(g * HEAD, HEAD)] = attended[g * PAD : (g + 1) * PAD]
    grad_store.wait()

    for i in range(4):
        core_copy(i).wait_send()
    for way in range(2):
        for ab in range(2):
            step1(0, ab, 0, way).wait_send()
            step1(1 + ab, ab, 1, way).wait_send()
            step2(ab, way).wait_send()
    for ab in range(2):
        step3(ab).wait_send()
    for d in range(1, 8):
        e2_copy(d).wait_send()
    for d in range(1, 16):
        e1(d).wait_send()
        kv(d).wait_send()
    for a in range(2):
        for b in range(8):
            if a + b:
                e3(a, b).wait_send()

    @pl.when(jnp.logical_not(lined))
    def _():
        e3(0, 0).wait_send()


def finish(w_ref, m_ref, v_ref, grad_ref, kv_ref, att_ref, nw_ref, nm_ref, nv_ref, nkv_ref, out_ref):
    nw_ref[...], nm_ref[...], nv_ref[...] = adam(w_ref[...], m_ref[...], v_ref[...], grad_ref[...])
    for s in range(STEPS):
        rows = slice(2 * s, 2 * s + 2)
        out_ref[s] = att_ref[rows, :].astype(BF16)
        for n in range(2):
            nkv_ref[n, s] = kv_ref[n, rows, :].astype(BF16)


def shards(
    learn_input,
    learn_cotangent,
    weight,
    moment,
    second,
    table,
    gain,
    query_weight,
    cache,
    token_ids,
    lengths,
):
    rows = lengths.shape[0]
    state = [one.reshape(2 * OWN, HEAD) for one in (weight, moment, second)]
    anywhere = pl.BlockSpec(memory_space=pl.ANY)
    vmem = pl.BlockSpec(memory_space=pltpu.VMEM)
    dma = pltpu.SemaphoreType.DMA
    grad, kv, att = pl.pallas_call(
        kernel,
        out_shape=(
            jax.ShapeDtypeStruct((2 * OWN, HEAD), F32),
            jax.ShapeDtypeStruct((2, PAD, HEAD), F32),
            jax.ShapeDtypeStruct((PAD, HEADS * HEAD), F32),
        ),
        in_specs=[anywhere] * 11,
        out_specs=(anywhere, vmem, vmem),
        scratch_shapes=[
            pltpu.VMEM((8, TOK, CHUNK), BF16),
            pltpu.VMEM((2 * TOK, HEAD), BF16),
            pltpu.VMEM((2 * TOK, HEAD), F32),
            pltpu.VMEM((2 * HEAD, TOK), BF16),
            pltpu.VMEM((3, 2 * OWN, HEAD), F32),
            pltpu.VMEM((VOCAB_OWN, CHUNK), BF16),
            pltpu.VMEM((WIDTH, HEADS * HEAD), BF16),
            pltpu.VMEM((2, 2, POSITIONS, HEAD), BF16),
            pltpu.VMEM((4, CHUNK, 2 * HEAD), BF16),
            pltpu.VMEM((4, CHUNK, 2 * HEAD), BF16),
            pltpu.VMEM((4, CHUNK, 2 * HEAD), F32),
            pltpu.VMEM((4, 2, CHUNK, HEAD), BF16),
            pltpu.VMEM((2, 2, 2, OWN, HEAD), BF16),
            pltpu.VMEM((2, 2, OWN, HEAD), BF16),
            pltpu.VMEM((2, 2, OWN, HEAD), BF16),
            pltpu.VMEM((2, OWN, HEAD), BF16),
            pltpu.VMEM((2, OWN, HEAD), BF16),
            pltpu.VMEM((16, 6 * PAD, HEAD), BF16),
            pltpu.VMEM((16, 6 * PAD, HEAD), BF16),
            pltpu.VMEM((8, 6 * PAD, HEAD), BF16),
            pltpu.VMEM((PAD, WIDTH), F32),
            pltpu.VMEM((PAD, HEADS * HEAD), F32),
            pltpu.VMEM((16, 4 * PAD, HEAD), BF16),
            pltpu.VMEM((3 * HEAD, 2 * HEAD), BF16),
            pltpu.VMEM((16, 2 * PAD, HEAD), BF16),
            pltpu.VMEM((16, 2 * PAD, HEAD), BF16),
            pltpu.VMEM((WIDTH // HEAD, HEAD), BF16),
            pltpu.VMEM((WIDTH // HEAD, HEAD), F32),
            pltpu.VMEM((STEPS, 32), jnp.int32),
            pltpu.SMEM((2,), jnp.int32),
            pltpu.VMEM((2 * OWN, HEAD), F32),
            dma((19,)),
            dma((2, 4)),
            dma((2, 2, 2, 2)),
            dma((2, 2, 2)),
            dma((2, 2)),
            dma((2, 16)),
            dma((2, 8)),
            dma((2, 16)),
            dma((2, 16)),
        ],
        compiler_params=pltpu.CompilerParams(
            collective_id=0, has_side_effects=True, vmem_limit_bytes=60 * 1024 * 1024
        ),
        name="step",
    )(
        learn_input,
        learn_cotangent.reshape(2 * TOK, HEAD),
        *state,
        table,
        gain.reshape(WIDTH // HEAD, HEAD),
        query_weight,
        cache.reshape(2, rows, POSITIONS, HEAD),
        token_ids.T,
        lengths,
    )
    like = jax.ShapeDtypeStruct((2 * OWN, HEAD), F32)
    *updated, new_kv, attended = pl.pallas_call(
        finish,
        out_shape=(
            like,
            like,
            like,
            jax.ShapeDtypeStruct((2, STEPS, 2, HEAD), BF16),
            jax.ShapeDtypeStruct((STEPS, 2, HEADS * HEAD), BF16),
        ),
        in_specs=[vmem] * 6,
        out_specs=(vmem,) * 5,
        name="finish",
    )(*state, grad, kv, att)
    new_weight, new_moment, new_second = (one.reshape(OWN, 2, HEAD) for one in updated)
    new_kv = new_kv.transpose(0, 2, 1, 3).reshape(2, rows, 1, STEPS, HEAD)
    attended = attended.transpose(1, 0, 2)
    return new_weight, new_moment, new_second, new_kv, attended


def solution(mesh):
    return jax.shard_map(
        shards,
        mesh=mesh,
        in_specs=(
            P(("group", "fsdp"), None),
            P(("group", "fsdp"), None, "tp"),
            P(("group", "fsdp"), None, "tp"),
            P(("group", "fsdp"), None, "tp"),
            P(("group", "fsdp"), None, "tp"),
            P(("group", "fsdp"), "tp"),
            P(),
            P(None, "tp"),
            P(None, ("group", "fsdp"), "tp", None, None),
            P(),
            P(("group", "fsdp")),
        ),
        out_specs=(
            P(("group", "fsdp"), None, "tp"),
            P(("group", "fsdp"), None, "tp"),
            P(("group", "fsdp"), None, "tp"),
            P(None, ("group", "fsdp"), "tp", None, None),
            P(("group", "fsdp"), None, "tp"),
        ),
        check_vma=False,
    )
```

```python
import math

import jax
import jax.numpy as jnp
from jax import lax
from jax.experimental import pallas as pl
from jax.experimental.pallas import tpu as pltpu
from jax.sharding import PartitionSpec as P

MESH = pl.DeviceIdType.MESH
BF16 = jnp.bfloat16
F32 = jnp.float32

WIDTH = 5120
TOK = 1024
HEAD = 128
HEADS = 8
STEPS = 3
VOCAB_OWN = 4864
POSITIONS = 4096
OWN = 320
CHUNK = 640
PAD = 8

learn_rate = 0.002
beta_one = 0.9
beta_two = 0.95
bias_one = 1.0 - 0.9**10
bias_two = 1.0 - 0.95**10
adam_eps = 1e-08
weight_decay = 0.1
norm_eps = 1e-06
rope_log = math.log(1000000.0)


def adam(weight, moment, second, grad):
    new_moment = beta_one * moment + (1.0 - beta_one) * grad
    new_second = beta_two * second + (1.0 - beta_two) * grad * grad
    update = new_moment / bias_one / (jnp.sqrt(new_second / bias_two) + adam_eps)
    new_weight = weight - learn_rate * (update + weight_decay * weight)
    return new_weight, new_moment, new_second


def head_norm(values):
    return values * lax.rsqrt(jnp.mean(values * values, axis=-1, keepdims=True) + norm_eps)


def kernel(
    li_hbm,
    cot_hbm,
    w_hbm,
    m_hbm,
    v_hbm,
    table_hbm,
    gain_hbm,
    qw_hbm,
    cache_hbm,
    ids_hbm,
    len_hbm,
    grad_hbm,
    kv_ref,
    att_ref,
    li,
    cot,
    cotf,
    cot_t,
    wm,
    table,
    qw,
    cache,
    core_send,
    core_recv,
    own,
    part,
    recv1,
    send2,
    recv2,
    send3,
    recv3,
    e1_send,
    e1_recv,
    e2,
    tiles,
    scaled,
    qraw,
    e3_send,
    e3_recv,
    fresh,
    kv_send,
    kv_recv,
    gain,
    gain32,
    ids,
    len_ref,
    grad,
    load_sem,
    core_sem,
    s1_sem,
    s2_sem,
    s3_sem,
    e1_sem,
    e2_sem,
    e3_sem,
    kv_sem,
):
    c, f, t = lax.axis_index("group"), lax.axis_index("fsdp"), lax.axis_index("tp")
    x, h = f // 2, f % 2
    gf = c * 8 + f
    other_c = 1 - c
    near_a = x + 1 - 2 * (x % 2)
    near_b = 3 - x
    far = (x + 2) % 4
    order = (far, near_a, near_b, x)

    core_peer = (other_c, f, t)
    a_peer = (c, near_a * 2 + h, t)
    b_peer = (c, near_b * 2 + h, t)
    h_peer = (c, x * 2 + 1 - h, t)

    def gf_peer(d):
        there = (gf + d) % 16
        return (there // 8, there % 8, t)

    def tp_peer(d):
        return (c, f, (t + d) % 8)

    def remote(src, dst, sems, index, peer):
        return pltpu.make_async_remote_copy(
            src_ref=src,
            dst_ref=dst,
            send_sem=sems.at[(0,) + index],
            recv_sem=sems.at[(1,) + index],
            device_id=peer,
            device_id_type=MESH,
        )

    def load(src, dst, n):
        return pltpu.make_async_copy(src, dst, load_sem.at[n])

    def li_load(j):
        core = other_c if j % 2 == 0 else c
        column = pl.multiple_of(core * 2560 + order[j // 2] * CHUNK, 128)
        return load(li_hbm.at[:, pl.ds(column, CHUNK)], li.at[j], j)

    cot_load = load(cot_hbm, cot, 8)
    table_load = load(table_hbm, table, 9)
    w_loads = [load(ref, wm.at[n], 10 + n) for n, ref in enumerate((w_hbm, m_hbm, v_hbm))]
    qw_load = load(qw_hbm, qw, 13)
    cache_load = load(cache_hbm, cache, 14)

    small_loads = [load(ids_hbm, ids, 15), load(len_hbm, len_ref, 16), load(gain_hbm, gain, 17)]

    cot_load.start()
    for one in small_loads:
        one.start()
    table_load.start()
    for j in range(8):
        li_load(j).start()

    barrier = pltpu.get_barrier_semaphore()
    for d in range(1, 16):
        pl.semaphore_signal(barrier, inc=1, device_id=gf_peer(d), device_id_type=MESH)
    for d in range(1, 8):
        pl.semaphore_signal(barrier, inc=1, device_id=tp_peer(d), device_id_type=MESH)

    cot_load.wait()
    cotf[...] = cot[...].astype(F32)
    for n in range(2):
        cot_t[pl.ds(n * HEAD, HEAD), :] = cotf[pl.ds(n, TOK, 2), :].T.astype(BF16)

    def term(j):
        li_load(j).wait()
        return jnp.dot(cot_t[...], li[j], preferred_element_type=F32).T

    def core_copy(i):
        return remote(core_send.at[i], core_recv.at[i], core_sem, (i,), core_peer)

    def terms(i):
        core_send[i] = term(2 * i).astype(BF16)
        if i == 0:
            pl.semaphore_wait(barrier, 22)
        core_copy(i).start()
        if i == 0:
            for d in range(1, 16):
                e1(d).start()
        own[i] = term(2 * i + 1)

    def add_cores(i):
        core_copy(i).wait_recv()
        for ab in range(2):
            lanes = pl.ds(ab * HEAD, HEAD)
            part[i, ab] = (own[i, :, lanes] + core_recv[i, :, lanes].astype(F32)).astype(BF16)

    def half(way):
        return pl.ds(pl.multiple_of((1 - h if way == 0 else h) * OWN, 64), OWN)

    peers = (a_peer, b_peer)

    def step1(i, ab, slot, way):
        return remote(
            part.at[i, ab, half(way)], recv1.at[ab, slot, way], s1_sem, (ab, slot, way), peers[ab]
        )

    def step2(ab, way):
        return remote(
            send2.at[ab, way], recv2.at[ab, way], s2_sem, (ab, way), peers[1 - ab]
        )

    def step2_go(way):
        for ab, i in ((0, 2), (1, 1)):
            step1(i, ab, 0, way).wait_recv()
            send2[ab, way] = (
                part[i, ab, half(way)].astype(F32) + recv1[ab, 0, way].astype(F32)
            ).astype(BF16)
            step2(ab, way).start()

    def step3(ab):
        return remote(send3.at[ab], recv3.at[ab], s3_sem, (ab,), h_peer)

    def x_sum(ab, way):
        step1(3, ab, 1, way).wait_recv()
        step2(ab, way).wait_recv()
        return (
            part[3, ab, half(way)].astype(F32)
            + recv1[ab, 1, way].astype(F32)
            + recv2[ab, way].astype(F32)
        )

    for one in small_loads:
        one.wait()
    slot = lax.broadcasted_iota(jnp.int32, (16 * PAD, 32), 0)
    row = lax.broadcasted_iota(jnp.int32, (16 * PAD, 32), 1)
    place = slot % PAD
    mine = row == 2 * (slot // PAD) + place % 2
    wanted = jnp.zeros((16 * PAD, 32), F32)
    for step in range(STEPS):
        here = mine & (place // 2 == step)
        wanted = wanted + jnp.where(here, ids[step : step + 1, :].astype(F32), 0.0)
    wanted = jnp.sum(wanted, axis=-1, keepdims=True).astype(jnp.int32)
    wanted = jnp.where(place[:, :1] < 2 * STEPS, wanted, -1)
    hot = jnp.where(
        lax.broadcasted_iota(jnp.int32, (16 * PAD, VOCAB_OWN), 1) == wanted - gf * VOCAB_OWN, 1.0, 0.0
    ).astype(BF16)
    table_load.wait()
    picked = jnp.dot(hot, table[...], preferred_element_type=F32)
    blank = jnp.zeros((PAD, HEAD), F32)
    for device in range(16):
        rows = picked[device * PAD : (device + 1) * PAD]
        e1_send[device] = jnp.concatenate(
            [rows[:, b * HEAD : (b + 1) * HEAD] for b in range(5)] + [blank], axis=0
        ).astype(BF16)

    def e1(d):
        return remote(e1_send.at[(gf + d) % 16], e1_recv.at[d], e1_sem, (d,), gf_peer(d))

    terms(0)
    qw_load.start()
    terms(1)
    add_cores(0)
    step1(0, 0, 0, 0).start()
    step1(0, 1, 0, 0).start()
    cache_load.start()
    for one in w_loads:
        one.start()
    terms(2)
    add_cores(1)
    step1(1, 0, 1, 0).start()
    terms(3)
    add_cores(2)
    step1(2, 1, 1, 0).start()
    add_cores(3)

    total = e1_send[gf].astype(F32)
    for d in range(1, 16):
        e1(d).wait_recv()
        total = total + e1_recv[d].astype(F32)
    e2[t] = total.astype(BF16)

    def e2_copy(d):
        return remote(e2.at[t], e2.at[t], e2_sem, (d,), tp_peer(d))

    def e2_arrival(d):
        there = (t + 8 - d) % 8
        return remote(e2.at[there], e2.at[there], e2_sem, (d,), tp_peer(d))

    for d in range(1, 8):
        e2_copy(d).start()

    step2_go(0)
    step1(0, 0, 0, 1).start()
    step1(0, 1, 0, 1).start()
    step1(1, 0, 1, 1).start()
    step1(2, 1, 1, 1).start()

    gain32[...] = gain[...].astype(F32)
    fresh[...] = jnp.zeros_like(fresh)
    tiles[pl.ds(40 * PAD, 2 * PAD), :] = jnp.zeros((2 * PAD, HEAD), F32)

    for ab in range(2):
        send3[ab] = x_sum(ab, 0).astype(BF16)
        step3(ab).start()

    for d in range(1, 8):
        e2_arrival(d).wait_recv()
    square = jnp.zeros((PAD, HEAD), F32)
    for n in range(8):
        emb = e2[n].astype(F32)
        for b in range(5):
            one = emb[b * PAD : (b + 1) * PAD]
            square = square + one * one
    mean = jnp.sum(square, axis=-1, keepdims=True) * (1.0 / WIDTH)
    factor = lax.rsqrt(mean + norm_eps)
    for n in range(8):
        emb = e2[n].astype(F32)
        for b in range(5):
            k = n * 5 + b
            one = emb[b * PAD : (b + 1) * PAD] * gain32[k : k + 1, :] * factor
            tiles[pl.ds(k * PAD, PAD), :] = one
            scaled[:, k * HEAD : (k + 1) * HEAD] = one

    def e3_block(device):
        first = (device // 2) * 5 + 2 * (device % 2)
        return tiles[pl.ds(pl.multiple_of(first * PAD, PAD), 4 * PAD), :].astype(BF16)

    for n in range(16):
        e3_send[n] = e3_block(n)

    def e3(d):
        return remote(e3_send.at[(gf + d) % 16], e3_recv.at[gf], e3_sem, (d,), gf_peer(d))

    def e3_arrival(d):
        there = (gf + 16 - d) % 16
        return remote(e3_send.at[there], e3_recv.at[there], e3_sem, (d,), gf_peer(d))

    for d in range(1, 16):
        e3(d).start()
    e3_recv[gf] = e3_send[gf]

    step2_go(1)

    qw_load.wait()
    scaled16 = scaled[...].astype(BF16)

    @pl.loop(0, 4)
    def _(n):
        columns = pl.ds(pl.multiple_of(n * 256, 256), 256)
        qraw[:, columns] = jnp.dot(scaled16, qw[:, columns], preferred_element_type=F32)

    place = lax.broadcasted_iota(jnp.int32, (PAD, HEAD), 0)
    lane = lax.broadcasted_iota(jnp.int32, (PAD, HEAD), 1)
    position = jnp.where(place % 2 == 0, len_ref[0], len_ref[1]) + place // 2
    freqs = jnp.exp((lane % (HEAD // 2)).astype(F32) * (-rope_log * 2.0 / HEAD))
    angles = position.astype(F32) * freqs
    cosine, sine = jnp.cos(angles), jnp.sin(angles)
    sine = jnp.where(lane < HEAD // 2, -sine, sine)

    def rotate(values):
        return values * cosine + pltpu.roll(values, HEAD // 2, 1) * sine

    query = jnp.concatenate(
        [
            rotate(head_norm(qraw[:, g * HEAD : (g + 1) * HEAD]))
            for g in range(HEADS)
        ],
        axis=0,
    ).astype(BF16)

    for d in range(1, 16):
        e3_arrival(d).wait_recv()
    arrived = [e3_recv[n].astype(F32) for n in range(16)]
    features = jnp.concatenate(
        [
            jnp.concatenate([one[b * PAD : (b + 1) * PAD] for one in arrived], axis=0)
            for b in range(3)
        ],
        axis=1,
    ).astype(BF16)

    for one in w_loads:
        one.wait()
    for ab in range(2):
        total = x_sum(ab, 1)
        step3(ab).wait_recv()
        total = total + recv3[ab].astype(F32)
        every = pl.ds(ab, OWN, 2)
        grad[every, :] = total
        new_weight, _, _ = adam(wm[0, every, :], wm[1, every, :], wm[2, every, :], total)
        fresh[pl.ds(pl.multiple_of(h * 64, 64), OWN), pl.ds(ab * HEAD, HEAD)] = new_weight.astype(
            BF16
        )
    partial = jnp.dot(features, fresh[...], preferred_element_type=F32)

    def kv(d):
        return remote(kv_send.at[(gf + d) % 16], kv_recv.at[d], kv_sem, (d,), gf_peer(d))

    for n in range(16):
        rows = partial[n * PAD : (n + 1) * PAD]
        kv_send[n] = jnp.concatenate([rows[:, :HEAD], rows[:, HEAD:]], axis=0).astype(BF16)
    for d in range(1, 16):
        kv(d).start()
    grad_store = load(grad, grad_hbm, 18)
    grad_store.start()

    scale = 1.0 / math.sqrt(HEAD)
    cache_load.wait()
    block = 1024
    sums = []
    for r in range(2):
        length = len_ref[r]

        def attend(n, carry, r=r, length=length):
            denom, numer = carry
            where = pl.ds(pl.multiple_of(n * block, block), block)
            scores = lax.dot_general(
                query, cache[0, r, where, :], (((1,), (1,)), ((), ())), preferred_element_type=F32
            )
            position = lax.broadcasted_iota(jnp.int32, scores.shape, 1) + n * block
            weights = jnp.where(position < length, jnp.exp(scores * scale), 0.0)
            denom = denom + jnp.sum(weights, axis=-1, keepdims=True)
            numer = numer + jnp.dot(
                weights.astype(BF16), cache[1, r, where, :], preferred_element_type=F32
            )
            return denom, numer

        rows = HEADS * PAD
        sums.append(
            lax.fori_loop(
                0,
                POSITIONS // block,
                attend,
                (jnp.zeros((rows, 1), F32), jnp.zeros((rows, HEAD), F32)),
            )
        )
    token = lax.broadcasted_iota(jnp.int32, (HEADS * PAD, 1), 0) % PAD
    first_row = token % 2 == 0
    denom = jnp.where(first_row, sums[0][0], sums[1][0])
    numer = jnp.where(first_row, sums[0][1], sums[1][1])

    total = kv_send[gf].astype(F32)
    for d in range(1, 16):
        kv(d).wait_recv()
        total = total + kv_recv[d].astype(F32)
    new_key = rotate(head_norm(total[:PAD])).astype(BF16).astype(F32)
    new_value = total[PAD:].astype(BF16).astype(F32)
    kv_ref[0] = new_key
    kv_ref[1] = new_value

    query32 = query.astype(F32)
    for j in range(2 * STEPS):
        score = jnp.sum(query32 * new_key[j : j + 1], axis=-1, keepdims=True) * scale
        seen = (token % 2 == j % 2) & (token >= j)
        weight = jnp.where(seen, jnp.exp(score), 0.0)
        denom = denom + weight
        numer = numer + weight.astype(BF16).astype(F32) * new_value[j : j + 1]
    attended = numer / denom
    for g in range(HEADS):
        att_ref[:, pl.ds(g * HEAD, HEAD)] = attended[g * PAD : (g + 1) * PAD]
    grad_store.wait()

    for i in range(4):
        core_copy(i).wait_send()
    for way in range(2):
        for ab in range(2):
            step1(0, ab, 0, way).wait_send()
            step1(1 + ab, ab, 1, way).wait_send()
            step2(ab, way).wait_send()
    for ab in range(2):
        step3(ab).wait_send()
    for d in range(1, 8):
        e2_copy(d).wait_send()
    for d in range(1, 16):
        e1(d).wait_send()
        e3(d).wait_send()
        kv(d).wait_send()


def finish(w_ref, m_ref, v_ref, grad_ref, kv_ref, att_ref, nw_ref, nm_ref, nv_ref, nkv_ref, out_ref):
    nw_ref[...], nm_ref[...], nv_ref[...] = adam(w_ref[...], m_ref[...], v_ref[...], grad_ref[...])
    for s in range(STEPS):
        rows = slice(2 * s, 2 * s + 2)
        out_ref[s] = att_ref[rows, :].astype(BF16)
        for n in range(2):
            nkv_ref[n, s] = kv_ref[n, rows, :].astype(BF16)


def shards(
    learn_input,
    learn_cotangent,
    weight,
    moment,
    second,
    table,
    gain,
    query_weight,
    cache,
    token_ids,
    lengths,
):
    rows = lengths.shape[0]
    state = [one.reshape(2 * OWN, HEAD) for one in (weight, moment, second)]
    anywhere = pl.BlockSpec(memory_space=pl.ANY)
    vmem = pl.BlockSpec(memory_space=pltpu.VMEM)
    dma = pltpu.SemaphoreType.DMA
    grad, kv, att = pl.pallas_call(
        kernel,
        out_shape=(
            jax.ShapeDtypeStruct((2 * OWN, HEAD), F32),
            jax.ShapeDtypeStruct((2, PAD, HEAD), F32),
            jax.ShapeDtypeStruct((PAD, HEADS * HEAD), F32),
        ),
        in_specs=[anywhere] * 11,
        out_specs=(anywhere, vmem, vmem),
        scratch_shapes=[
            pltpu.VMEM((8, TOK, CHUNK), BF16),
            pltpu.VMEM((2 * TOK, HEAD), BF16),
            pltpu.VMEM((2 * TOK, HEAD), F32),
            pltpu.VMEM((2 * HEAD, TOK), BF16),
            pltpu.VMEM((3, 2 * OWN, HEAD), F32),
            pltpu.VMEM((VOCAB_OWN, CHUNK), BF16),
            pltpu.VMEM((WIDTH, HEADS * HEAD), BF16),
            pltpu.VMEM((2, 2, POSITIONS, HEAD), BF16),
            pltpu.VMEM((4, CHUNK, 2 * HEAD), BF16),
            pltpu.VMEM((4, CHUNK, 2 * HEAD), BF16),
            pltpu.VMEM((4, CHUNK, 2 * HEAD), F32),
            pltpu.VMEM((4, 2, CHUNK, HEAD), BF16),
            pltpu.VMEM((2, 2, 2, OWN, HEAD), BF16),
            pltpu.VMEM((2, 2, OWN, HEAD), BF16),
            pltpu.VMEM((2, 2, OWN, HEAD), BF16),
            pltpu.VMEM((2, OWN, HEAD), BF16),
            pltpu.VMEM((2, OWN, HEAD), BF16),
            pltpu.VMEM((16, 6 * PAD, HEAD), BF16),
            pltpu.VMEM((16, 6 * PAD, HEAD), BF16),
            pltpu.VMEM((8, 6 * PAD, HEAD), BF16),
            pltpu.VMEM((42 * PAD, HEAD), F32),
            pltpu.VMEM((PAD, WIDTH), F32),
            pltpu.VMEM((PAD, HEADS * HEAD), F32),
            pltpu.VMEM((16, 4 * PAD, HEAD), BF16),
            pltpu.VMEM((16, 4 * PAD, HEAD), BF16),
            pltpu.VMEM((3 * HEAD, 2 * HEAD), BF16),
            pltpu.VMEM((16, 2 * PAD, HEAD), BF16),
            pltpu.VMEM((16, 2 * PAD, HEAD), BF16),
            pltpu.VMEM((WIDTH // HEAD, HEAD), BF16),
            pltpu.VMEM((WIDTH // HEAD, HEAD), F32),
            pltpu.VMEM((STEPS, 32), jnp.int32),
            pltpu.SMEM((2,), jnp.int32),
            pltpu.VMEM((2 * OWN, HEAD), F32),
            dma((19,)),
            dma((2, 4)),
            dma((2, 2, 2, 2)),
            dma((2, 2, 2)),
            dma((2, 2)),
            dma((2, 16)),
            dma((2, 8)),
            dma((2, 16)),
            dma((2, 16)),
        ],
        compiler_params=pltpu.CompilerParams(
            collective_id=0, has_side_effects=True, vmem_limit_bytes=60 * 1024 * 1024
        ),
        name="step",
    )(
        learn_input,
        learn_cotangent.reshape(2 * TOK, HEAD),
        *state,
        table,
        gain.reshape(WIDTH // HEAD, HEAD),
        query_weight,
        cache.reshape(2, rows, POSITIONS, HEAD),
        token_ids.T,
        lengths,
    )
    like = jax.ShapeDtypeStruct((2 * OWN, HEAD), F32)
    *updated, new_kv, attended = pl.pallas_call(
        finish,
        out_shape=(
            like,
            like,
            like,
            jax.ShapeDtypeStruct((2, STEPS, 2, HEAD), BF16),
            jax.ShapeDtypeStruct((STEPS, 2, HEADS * HEAD), BF16),
        ),
        in_specs=[vmem] * 6,
        out_specs=(vmem,) * 5,
        name="finish",
    )(*state, grad, kv, att)
    new_weight, new_moment, new_second = (one.reshape(OWN, 2, HEAD) for one in updated)
    new_kv = new_kv.transpose(0, 2, 1, 3).reshape(2, rows, 1, STEPS, HEAD)
    attended = attended.transpose(1, 0, 2)
    return new_weight, new_moment, new_second, new_kv, attended


def solution(mesh):
    return jax.shard_map(
        shards,
        mesh=mesh,
        in_specs=(
            P(("group", "fsdp"), None),
            P(("group", "fsdp"), None, "tp"),
            P(("group", "fsdp"), None, "tp"),
            P(("group", "fsdp"), None, "tp"),
            P(("group", "fsdp"), None, "tp"),
            P(("group", "fsdp"), "tp"),
            P(),
            P(None, "tp"),
            P(None, ("group", "fsdp"), "tp", None, None),
            P(),
            P(("group", "fsdp")),
        ),
        out_specs=(
            P(("group", "fsdp"), None, "tp"),
            P(("group", "fsdp"), None, "tp"),
            P(("group", "fsdp"), None, "tp"),
            P(None, ("group", "fsdp"), "tp", None, None),
            P(("group", "fsdp"), None, "tp"),
        ),
        check_vma=False,
    )
```

```python
import math

import jax
import jax.numpy as jnp
from jax import lax
from jax.experimental import pallas as pl
from jax.experimental.pallas import tpu as pltpu
from jax.sharding import PartitionSpec as P

MESH = pl.DeviceIdType.MESH
BF16 = jnp.bfloat16
F32 = jnp.float32

WIDTH = 5120
TOK = 1024
HEAD = 128
HEADS = 8
STEPS = 3
VOCAB_OWN = 4864
POSITIONS = 4096
OWN = 320
CHUNK = 640
TOKENS = 6
PAD = 8
ROWS = 32

learn_rate = 0.002
beta_one = 0.9
beta_two = 0.95
bias_one = 1.0 - 0.9**10
bias_two = 1.0 - 0.95**10
adam_eps = 1e-08
weight_decay = 0.1
norm_eps = 1e-06
rope_log = math.log(1000000.0)


def adam(weight, moment, second, grad):
    new_moment = beta_one * moment + (1.0 - beta_one) * grad
    new_second = beta_two * second + (1.0 - beta_two) * grad * grad
    update = new_moment / bias_one / (jnp.sqrt(new_second / bias_two) + adam_eps)
    new_weight = weight - learn_rate * (update + weight_decay * weight)
    return new_weight, new_moment, new_second


def head_norm(values):
    return values * lax.rsqrt(jnp.mean(values * values, axis=-1, keepdims=True) + norm_eps)


def kernel(
    li_hbm,
    cot_hbm,
    w_hbm,
    m_hbm,
    v_hbm,
    table_hbm,
    gain_hbm,
    qw_hbm,
    cache_hbm,
    ids_hbm,
    len_hbm,
    nw_hbm,
    nm_hbm,
    nv_hbm,
    kv_ref,
    att_ref,
    li,
    cot,
    cotf,
    cot_t,
    wm,
    table,
    qw,
    cache,
    core_send,
    core_recv,
    own,
    part,
    recv1,
    send2,
    recv2,
    send3,
    recv3,
    e1_pack,
    e1_send,
    e1_recv,
    e2,
    e2_wide,
    scaled,
    qraw,
    e3_recv,
    e3_wide,
    fresh,
    kv_send,
    kv_recv,
    gain,
    gain32,
    ids,
    len_ref,
    updated,
    load_sem,
    core_sem,
    s1_sem,
    s2_sem,
    s3_sem,
    e1_sem,
    e2_sem,
    e3_sem,
    kv_sem,
):
    c, f, t = lax.axis_index("group"), lax.axis_index("fsdp"), lax.axis_index("tp")
    x, h = f // 2, f % 2
    gf = c * 8 + f
    other_c = 1 - c
    near_a = x + 1 - 2 * (x % 2)
    near_b = 3 - x
    far = (x + 2) % 4
    order = (far, near_a, near_b, x)

    core_peer = (other_c, f, t)
    a_peer = (c, near_a * 2 + h, t)
    b_peer = (c, near_b * 2 + h, t)
    h_peer = (c, x * 2 + 1 - h, t)

    def gf_peer(d):
        there = (gf + d) % 16
        return (there // 8, there % 8, t)

    def tp_peer(d):
        return (c, f, (t + d) % 8)

    def remote(src, dst, sems, index, peer):
        return pltpu.make_async_remote_copy(
            src_ref=src,
            dst_ref=dst,
            send_sem=sems.at[(0,) + index],
            recv_sem=sems.at[(1,) + index],
            device_id=peer,
            device_id_type=MESH,
        )

    def load(src, dst, n):
        return pltpu.make_async_copy(src, dst, load_sem.at[n])

    def li_load(j):
        core = other_c if j % 2 == 0 else c
        column = pl.multiple_of(core * 2560 + order[j // 2] * CHUNK, 128)
        return load(li_hbm.at[:, pl.ds(column, CHUNK)], li.at[j], j)

    cot_load = load(cot_hbm, cot, 8)
    part_rows = VOCAB_OWN // 2
    table_parts = [pl.ds(n * part_rows, part_rows) for n in range(2)]
    table_loads = [
        load(table_hbm.at[rows], table.at[rows], n) for rows, n in zip(table_parts, (9, 21))
    ]
    w_loads = [load(ref, wm.at[n], 10 + n) for n, ref in enumerate((w_hbm, m_hbm, v_hbm))]
    qw_load = load(qw_hbm, qw, 13)
    cache_load = load(cache_hbm, cache, 14)

    small_loads = [load(ids_hbm, ids, 15), load(len_hbm, len_ref, 16), load(gain_hbm, gain, 17)]

    cot_load.start()
    for one in small_loads:
        one.start()
    for one in table_loads:
        one.start()
    for j in range(8):
        li_load(j).start()

    barrier = pltpu.get_barrier_semaphore()
    for d in range(1, 16):
        pl.semaphore_signal(barrier, inc=1, device_id=gf_peer(d), device_id_type=MESH)
    for d in range(1, 8):
        pl.semaphore_signal(barrier, inc=1, device_id=tp_peer(d), device_id_type=MESH)

    cot_load.wait()
    cotf[...] = cot[...].astype(F32)
    for n in range(2):
        cot_t[pl.ds(n * HEAD, HEAD), :] = cotf[pl.ds(n, TOK, 2), :].T.astype(BF16)

    def term(j):
        li_load(j).wait()
        return jnp.dot(cot_t[...], li[j], preferred_element_type=F32).T

    def core_copy(i):
        return remote(core_send.at[i], core_recv.at[i], core_sem, (i,), core_peer)

    def terms(i):
        core_send[i] = term(2 * i).astype(BF16)
        if i == 0:
            pl.semaphore_wait(barrier, 22)
        core_copy(i).start()
        if i == 0:
            for d in range(1, 16):
                e1(d).start()
        own[i] = term(2 * i + 1)

    def add_cores(i):
        core_copy(i).wait_recv()
        for ab in range(2):
            lanes = pl.ds(ab * HEAD, HEAD)
            part[i, ab] = (own[i, :, lanes] + core_recv[i, :, lanes].astype(F32)).astype(BF16)

    def half(way):
        return pl.ds(pl.multiple_of((1 - h if way == 0 else h) * OWN, 64), OWN)

    peers = (a_peer, b_peer)

    def step1(i, ab, slot, way):
        return remote(
            part.at[i, ab, half(way)], recv1.at[ab, slot, way], s1_sem, (ab, slot, way), peers[ab]
        )

    def step2(ab, way):
        return remote(
            send2.at[ab, way], recv2.at[ab, way], s2_sem, (ab, way), peers[1 - ab]
        )

    def step2_go(way):
        for ab, i in ((0, 2), (1, 1)):
            step1(i, ab, 0, way).wait_recv()
            send2[ab, way] = (
                part[i, ab, half(way)].astype(F32) + recv1[ab, 0, way].astype(F32)
            ).astype(BF16)
            step2(ab, way).start()

    def step3(ab):
        return remote(send3.at[ab], recv3.at[ab], s3_sem, (ab,), h_peer)

    def x_sum(ab, way):
        step1(3, ab, 1, way).wait_recv()
        step2(ab, way).wait_recv()
        return (
            part[3, ab, half(way)].astype(F32)
            + recv1[ab, 1, way].astype(F32)
            + recv2[ab, way].astype(F32)
        )

    for one in small_loads:
        one.wait()
    slot = lax.broadcasted_iota(jnp.int32, (16 * PAD, 32), 0)
    row = lax.broadcasted_iota(jnp.int32, (16 * PAD, 32), 1)
    place = slot % PAD
    mine = row == 2 * (slot // PAD) + place % 2
    wanted = jnp.zeros((16 * PAD, 32), F32)
    for step in range(STEPS):
        here = mine & (place // 2 == step)
        wanted = wanted + jnp.where(here, ids[step : step + 1, :].astype(F32), 0.0)
    wanted = jnp.sum(wanted, axis=-1, keepdims=True).astype(jnp.int32)
    wanted = jnp.where(place[:, :1] < 2 * STEPS, wanted, -1)
    hot = jnp.where(
        lax.broadcasted_iota(jnp.int32, (16 * PAD, VOCAB_OWN), 1) == wanted - gf * VOCAB_OWN, 1.0, 0.0
    ).astype(BF16)
    picked = jnp.zeros((16 * PAD, CHUNK), F32)
    for n in range(2):
        table_loads[n].wait()
        columns = slice(n * part_rows, (n + 1) * part_rows)
        picked = picked + jnp.dot(
            hot[:, columns], table[table_parts[n], :], preferred_element_type=F32
        )
    e1_pack[...] = jnp.zeros_like(e1_pack)
    for device in range(16):
        for b in range(5):
            e1_pack[device, b * TOKENS : (b + 1) * TOKENS, :] = picked[
                device * PAD : device * PAD + TOKENS, b * HEAD : (b + 1) * HEAD
            ]
    e1_send[...] = e1_pack[...].astype(BF16)

    def e1(d):
        return remote(e1_send.at[(gf + d) % 16], e1_recv.at[d], e1_sem, (d,), gf_peer(d))

    terms(0)
    qw_load.start()
    terms(1)
    add_cores(0)
    step1(0, 0, 0, 0).start()
    step1(0, 1, 0, 0).start()
    cache_load.start()
    for one in w_loads:
        one.start()
    terms(2)
    add_cores(1)
    step1(1, 0, 1, 0).start()
    terms(3)
    add_cores(2)
    step1(2, 1, 1, 0).start()
    add_cores(3)

    total = e1_send[gf].astype(F32)
    for d in range(1, 16):
        e1(d).wait_recv()
        total = total + e1_recv[d].astype(F32)
    e2[t] = total.astype(BF16)

    def e2_copy(d):
        return remote(e2.at[t], e2.at[t], e2_sem, (d,), tp_peer(d))

    def e2_arrival(d):
        there = (t + 8 - d) % 8
        return remote(e2.at[there], e2.at[there], e2_sem, (d,), tp_peer(d))

    for d in range(1, 8):
        e2_copy(d).start()

    def e3(d, a):
        source = (t + 8 - d) % 8
        to = 2 * source + (h + a) % 2
        return pltpu.make_async_remote_copy(
            src_ref=e2.at[source],
            dst_ref=e3_recv.at[gf],
            send_sem=e3_sem.at[0, 2 * d + a],
            recv_sem=e3_sem.at[1, gf],
            device_id=(to // 8, to % 8, t),
            device_id_type=MESH,
        )

    def e3_arrival(d):
        there = (gf + d) % 16
        return pltpu.make_async_remote_copy(
            src_ref=e2.at[0],
            dst_ref=e3_recv.at[there],
            send_sem=e3_sem.at[0, 0],
            recv_sem=e3_sem.at[1, there],
            device_id=gf_peer(d),
            device_id_type=MESH,
        )

    def itself(d):
        return (t + 8 - d) % 8 == gf // 2

    def e3_go(d):
        e3(d, 1).start()

        @pl.when(jnp.logical_not(itself(d)))
        def _():
            e3(d, 0).start()

        @pl.when(itself(d))
        def _():
            e3_recv[gf] = e2[gf // 2]

    e3_go(0)
    step2_go(0)
    step1(0, 0, 0, 1).start()
    step1(0, 1, 0, 1).start()
    step1(1, 0, 1, 1).start()
    step1(2, 1, 1, 1).start()
    gain32[...] = gain[...].astype(F32)
    fresh[...] = jnp.zeros_like(fresh)
    for ab in range(2):
        send3[ab] = x_sum(ab, 0).astype(BF16)
        step3(ab).start()
    for d in (1, 7, 2, 6, 3, 5, 4):
        e2_arrival(d).wait_recv()
        e3_go(d)
    step2_go(1)
    for n in range(8):
        e2_wide[n] = e2[n].astype(F32)
    square = jnp.zeros((PAD, HEAD), F32)
    for n in range(8):
        for b in range(5):
            one = e2_wide[n, pl.ds(b * TOKENS, PAD), :]
            square = square + one * one
    mean = jnp.sum(square, axis=-1, keepdims=True) * (1.0 / WIDTH)
    factor = lax.rsqrt(mean + norm_eps)
    for n in range(8):
        for b in range(5):
            k = n * 5 + b
            one = e2_wide[n, pl.ds(b * TOKENS, PAD), :] * gain32[k : k + 1, :] * factor
            scaled[:, k * HEAD : (k + 1) * HEAD] = one

    qw_load.wait()
    scaled16 = scaled[...].astype(BF16)

    @pl.loop(0, 4)
    def _(n):
        columns = pl.ds(pl.multiple_of(n * 256, 256), 256)
        qraw[:, columns] = jnp.dot(scaled16, qw[:, columns], preferred_element_type=F32)

    place = lax.broadcasted_iota(jnp.int32, (PAD, HEAD), 0)
    lane = lax.broadcasted_iota(jnp.int32, (PAD, HEAD), 1)
    position = jnp.where(place % 2 == 0, len_ref[0], len_ref[1]) + place // 2
    freqs = jnp.exp((lane % (HEAD // 2)).astype(F32) * (-rope_log * 2.0 / HEAD))
    angles = position.astype(F32) * freqs
    cosine, sine = jnp.cos(angles), jnp.sin(angles)
    sine = jnp.where(lane < HEAD // 2, -sine, sine)

    def rotate(values):
        return values * cosine + pltpu.roll(values, HEAD // 2, 1) * sine

    query = jnp.concatenate(
        [
            rotate(head_norm(qraw[:, g * HEAD : (g + 1) * HEAD]))
            for g in range(HEADS)
        ],
        axis=0,
    ).astype(BF16)

    scale = 1.0 / math.sqrt(HEAD)
    block = 1024

    def attend(r):
        length = len_ref[r]

        def step(n, carry):
            denom, numer = carry
            where = pl.ds(pl.multiple_of(n * block, block), block)
            scores = lax.dot_general(
                query, cache[0, r, where, :], (((1,), (1,)), ((), ())), preferred_element_type=F32
            )
            position = lax.broadcasted_iota(jnp.int32, scores.shape, 1) + n * block
            weights = jnp.where(position < length, jnp.exp(scores * scale), 0.0)
            denom = denom + jnp.sum(weights, axis=-1, keepdims=True)
            numer = numer + jnp.dot(
                weights.astype(BF16), cache[1, r, where, :], preferred_element_type=F32
            )
            return denom, numer

        rows = HEADS * PAD
        return lax.fori_loop(
            0,
            POSITIONS // block,
            step,
            (jnp.zeros((rows, 1), F32), jnp.zeros((rows, HEAD), F32)),
        )

    cache_load.wait()
    first_sums = attend(0)

    for d in range(1, 16):
        e3_arrival(d).wait_recv()
    e3_wide[...] = e3_recv[...].astype(F32)
    first = (gf // 2) * 5 + 2 * h
    columns = []
    for b in range(3):
        low, high = [
            jnp.concatenate(
                [e3_wide[n, pl.ds((b + start) * TOKENS, PAD), :] for n in range(16)], axis=0
            )
            for start in (0, 2)
        ]
        columns.append(jnp.where(h == 0, low, high) * gain32[pl.ds(first + b, 1), :])
    features = jnp.concatenate(columns, axis=1).astype(BF16)

    for one in w_loads:
        one.wait()
    for ab in range(2):
        total = x_sum(ab, 1)
        step3(ab).wait_recv()
        total = total + recv3[ab].astype(F32)
        every = pl.ds(ab, OWN, 2)
        new_weight, new_moment, new_second = adam(
            wm[0, every, :], wm[1, every, :], wm[2, every, :], total
        )
        updated[0, every, :] = new_weight
        updated[1, every, :] = new_moment
        updated[2, every, :] = new_second
        fresh[pl.ds(pl.multiple_of(h * 64, 64), OWN), pl.ds(ab * HEAD, HEAD)] = new_weight.astype(
            BF16
        )
    partial = jnp.dot(features, fresh[...], preferred_element_type=F32)

    def kv(d):
        return remote(kv_send.at[(gf + d) % 16], kv_recv.at[d], kv_sem, (d,), gf_peer(d))

    for n in range(16):
        rows = partial[n * PAD : (n + 1) * PAD]
        kv_send[n] = jnp.concatenate([rows[:, :HEAD], rows[:, HEAD:]], axis=0).astype(BF16)
    for d in range(1, 16):
        kv(d).start()
    stores = [load(updated.at[n], ref, 18 + n) for n, ref in enumerate((nw_hbm, nm_hbm, nv_hbm))]
    for one in stores:
        one.start()

    second_sums = attend(1)
    token = lax.broadcasted_iota(jnp.int32, (HEADS * PAD, 1), 0) % PAD
    first_row = token % 2 == 0
    denom = jnp.where(first_row, first_sums[0], second_sums[0])
    numer = jnp.where(first_row, first_sums[1], second_sums[1])

    total = kv_send[gf].astype(F32)
    for d in range(1, 16):
        kv(d).wait_recv()
        total = total + kv_recv[d].astype(F32)
    new_key = rotate(head_norm(total[:PAD] * factor)).astype(BF16).astype(F32)
    new_value = (total[PAD:] * factor).astype(BF16).astype(F32)
    kv_ref[0] = new_key
    kv_ref[1] = new_value

    query32 = query.astype(F32)
    for j in range(2 * STEPS):
        score = jnp.sum(query32 * new_key[j : j + 1], axis=-1, keepdims=True) * scale
        seen = (token % 2 == j % 2) & (token >= j)
        weight = jnp.where(seen, jnp.exp(score), 0.0)
        denom = denom + weight
        numer = numer + weight.astype(BF16).astype(F32) * new_value[j : j + 1]
    attended = numer / denom
    for g in range(HEADS):
        att_ref[:, pl.ds(g * HEAD, HEAD)] = attended[g * PAD : (g + 1) * PAD]
    for one in stores:
        one.wait()

    for i in range(4):
        core_copy(i).wait_send()
    for way in range(2):
        for ab in range(2):
            step1(0, ab, 0, way).wait_send()
            step1(1 + ab, ab, 1, way).wait_send()
            step2(ab, way).wait_send()
    for ab in range(2):
        step3(ab).wait_send()
    for d in range(1, 8):
        e2_copy(d).wait_send()
    for d in range(1, 16):
        e1(d).wait_send()
        kv(d).wait_send()
    for d in range(8):
        e3(d, 1).wait_send()

        @pl.when(jnp.logical_not(itself(d)))
        def _(d=d):
            e3(d, 0).wait_send()


def finish(w_in, m_in, v_in, kv_in, att_in, w_out, m_out, v_out, kv_out, att_out, state, kv, att, new_kv, out, sem):
    def copy(src, dst, n):
        return pltpu.make_async_copy(src, dst, sem.at[n])

    loads = [copy(kv_in, kv, 0), copy(att_in, att, 1)]
    moves = [copy(ref, state.at[n], 2 + n) for n, ref in enumerate((w_in, m_in, v_in))]
    stores = [copy(state.at[n], ref, 5 + n) for n, ref in enumerate((w_out, m_out, v_out))]
    for one in loads + moves:
        one.start()
    for one in loads:
        one.wait()
    for s in range(STEPS):
        rows = slice(2 * s, 2 * s + 2)
        out[s] = att[rows, :].astype(BF16)
        for n in range(2):
            new_kv[n, s] = kv[n, rows, :].astype(BF16)
    small = [copy(new_kv, kv_out, 8), copy(out, att_out, 9)]
    for one in small:
        one.start()
    for load, store in zip(moves, stores):
        load.wait()
        store.start()
    for one in small + stores:
        one.wait()


def shards(
    learn_input,
    learn_cotangent,
    weight,
    moment,
    second,
    table,
    gain,
    query_weight,
    cache,
    token_ids,
    lengths,
):
    rows = lengths.shape[0]
    state = [one.reshape(2 * OWN, HEAD) for one in (weight, moment, second)]
    anywhere = pl.BlockSpec(memory_space=pl.ANY)
    vmem = pl.BlockSpec(memory_space=pltpu.VMEM)
    dma = pltpu.SemaphoreType.DMA
    like = jax.ShapeDtypeStruct((2 * OWN, HEAD), F32)
    *updated, kv, att = pl.pallas_call(
        kernel,
        out_shape=(
            like,
            like,
            like,
            jax.ShapeDtypeStruct((2, PAD, HEAD), F32),
            jax.ShapeDtypeStruct((PAD, HEADS * HEAD), F32),
        ),
        in_specs=[anywhere] * 11,
        out_specs=(anywhere,) * 3 + (vmem, vmem),
        scratch_shapes=[
            pltpu.VMEM((8, TOK, CHUNK), BF16),
            pltpu.VMEM((2 * TOK, HEAD), BF16),
            pltpu.VMEM((2 * TOK, HEAD), F32),
            pltpu.VMEM((2 * HEAD, TOK), BF16),
            pltpu.VMEM((3, 2 * OWN, HEAD), F32),
            pltpu.VMEM((VOCAB_OWN, CHUNK), BF16),
            pltpu.VMEM((WIDTH, HEADS * HEAD), BF16),
            pltpu.VMEM((2, 2, POSITIONS, HEAD), BF16),
            pltpu.VMEM((4, CHUNK, 2 * HEAD), BF16),
            pltpu.VMEM((4, CHUNK, 2 * HEAD), BF16),
            pltpu.VMEM((4, CHUNK, 2 * HEAD), F32),
            pltpu.VMEM((4, 2, CHUNK, HEAD), BF16),
            pltpu.VMEM((2, 2, 2, OWN, HEAD), BF16),
            pltpu.VMEM((2, 2, OWN, HEAD), BF16),
            pltpu.VMEM((2, 2, OWN, HEAD), BF16),
            pltpu.VMEM((2, OWN, HEAD), BF16),
            pltpu.VMEM((2, OWN, HEAD), BF16),
            pltpu.VMEM((16, ROWS, HEAD), F32),
            pltpu.VMEM((16, ROWS, HEAD), BF16),
            pltpu.VMEM((16, ROWS, HEAD), BF16),
            pltpu.VMEM((8, ROWS, HEAD), BF16),
            pltpu.VMEM((8, ROWS, HEAD), F32),
            pltpu.VMEM((PAD, WIDTH), F32),
            pltpu.VMEM((PAD, HEADS * HEAD), F32),
            pltpu.VMEM((16, ROWS, HEAD), BF16),
            pltpu.VMEM((16, ROWS, HEAD), F32),
            pltpu.VMEM((3 * HEAD, 2 * HEAD), BF16),
            pltpu.VMEM((16, 2 * PAD, HEAD), BF16),
            pltpu.VMEM((16, 2 * PAD, HEAD), BF16),
            pltpu.VMEM((WIDTH // HEAD, HEAD), BF16),
            pltpu.VMEM((WIDTH // HEAD, HEAD), F32),
            pltpu.VMEM((STEPS, 32), jnp.int32),
            pltpu.SMEM((2,), jnp.int32),
            pltpu.VMEM((3, 2 * OWN, HEAD), F32),
            dma((22,)),
            dma((2, 4)),
            dma((2, 2, 2, 2)),
            dma((2, 2, 2)),
            dma((2, 2)),
            dma((2, 16)),
            dma((2, 8)),
            dma((2, 16)),
            dma((2, 16)),
        ],
        compiler_params=pltpu.CompilerParams(
            collective_id=0, has_side_effects=True, vmem_limit_bytes=60 * 1024 * 1024
        ),
        name="step",
    )(
        learn_input,
        learn_cotangent.reshape(2 * TOK, HEAD),
        *state,
        table,
        gain.reshape(WIDTH // HEAD, HEAD),
        query_weight,
        cache.reshape(2, rows, POSITIONS, HEAD),
        token_ids.T,
        lengths,
    )
    *updated, new_kv, attended = pl.pallas_call(
        finish,
        out_shape=(
            like,
            like,
            like,
            jax.ShapeDtypeStruct((2, STEPS, 2, HEAD), BF16),
            jax.ShapeDtypeStruct((STEPS, 2, HEADS * HEAD), BF16),
        ),
        in_specs=[anywhere] * 5,
        out_specs=(anywhere,) * 5,
        scratch_shapes=[
            pltpu.VMEM((3, 2 * OWN, HEAD), F32),
            pltpu.VMEM((2, PAD, HEAD), F32),
            pltpu.VMEM((PAD, HEADS * HEAD), F32),
            pltpu.VMEM((2, STEPS, 2, HEAD), BF16),
            pltpu.VMEM((STEPS, 2, HEADS * HEAD), BF16),
            dma((10,)),
        ],
        name="finish",
    )(*updated, kv, att)
    new_weight, new_moment, new_second = (one.reshape(OWN, 2, HEAD) for one in updated)
    new_kv = new_kv.transpose(0, 2, 1, 3).reshape(2, rows, 1, STEPS, HEAD)
    attended = attended.transpose(1, 0, 2)
    return new_weight, new_moment, new_second, new_kv, attended


def solution(mesh):
    return jax.shard_map(
        shards,
        mesh=mesh,
        in_specs=(
            P(("group", "fsdp"), None),
            P(("group", "fsdp"), None, "tp"),
            P(("group", "fsdp"), None, "tp"),
            P(("group", "fsdp"), None, "tp"),
            P(("group", "fsdp"), None, "tp"),
            P(("group", "fsdp"), "tp"),
            P(),
            P(None, "tp"),
            P(None, ("group", "fsdp"), "tp", None, None),
            P(),
            P(("group", "fsdp")),
        ),
        out_specs=(
            P(("group", "fsdp"), None, "tp"),
            P(("group", "fsdp"), None, "tp"),
            P(("group", "fsdp"), None, "tp"),
            P(None, ("group", "fsdp"), "tp", None, None),
            P(("group", "fsdp"), None, "tp"),
        ),
        check_vma=False,
    )
```

```python
import math

import jax
import jax.numpy as jnp
from jax import lax
from jax.experimental import pallas as pl
from jax.experimental.pallas import tpu as pltpu
from jax.sharding import PartitionSpec as P

MESH = pl.DeviceIdType.MESH
BF16 = jnp.bfloat16
F32 = jnp.float32

WIDTH = 5120
TOK = 1024
HEAD = 128
HEADS = 8
STEPS = 3
VOCAB_OWN = 4864
POSITIONS = 4096
OWN = 320
CHUNK = 640
TOKENS = 6
PAD = 8
ROWS = 32

learn_rate = 0.002
beta_one = 0.9
beta_two = 0.95
bias_one = 1.0 - 0.9**10
bias_two = 1.0 - 0.95**10
adam_eps = 1e-08
weight_decay = 0.1
norm_eps = 1e-06
rope_log = math.log(1000000.0)


def adam(weight, moment, second, grad):
    new_moment = beta_one * moment + (1.0 - beta_one) * grad
    new_second = beta_two * second + (1.0 - beta_two) * grad * grad
    update = new_moment / bias_one / (jnp.sqrt(new_second / bias_two) + adam_eps)
    new_weight = weight - learn_rate * (update + weight_decay * weight)
    return new_weight, new_moment, new_second


def head_norm(values):
    return values * lax.rsqrt(jnp.mean(values * values, axis=-1, keepdims=True) + norm_eps)


def kernel(
    li_hbm,
    cot_hbm,
    w_hbm,
    m_hbm,
    v_hbm,
    table_hbm,
    gain_hbm,
    qw_hbm,
    cache_hbm,
    ids_hbm,
    len_hbm,
    nw_hbm,
    nm_hbm,
    nv_hbm,
    kv_ref,
    att_ref,
    li,
    cot,
    cotf,
    cot_t,
    wm,
    table,
    qw,
    cache,
    core_send,
    core_recv,
    own,
    part,
    recv1,
    send2,
    recv2,
    send3,
    recv3,
    e1_pack,
    e1_send,
    e1_recv,
    e2,
    e2_wide,
    scaled,
    qraw,
    e3_recv,
    e3_wide,
    fresh,
    kv_send,
    kv_recv,
    gain,
    gain32,
    ids,
    len_ref,
    updated,
    load_sem,
    core_sem,
    s1_sem,
    s2_sem,
    s3_sem,
    e1_sem,
    e2_sem,
    e3_sem,
    kv_sem,
):
    c, f, t = lax.axis_index("group"), lax.axis_index("fsdp"), lax.axis_index("tp")
    x, h = f // 2, f % 2
    gf = c * 8 + f
    other_c = 1 - c
    near_a = x + 1 - 2 * (x % 2)
    near_b = 3 - x
    far = (x + 2) % 4
    order = (far, near_a, near_b, x)

    core_peer = (other_c, f, t)
    a_peer = (c, near_a * 2 + h, t)
    b_peer = (c, near_b * 2 + h, t)
    h_peer = (c, x * 2 + 1 - h, t)

    def gf_peer(d):
        there = (gf + d) % 16
        return (there // 8, there % 8, t)

    def tp_peer(d):
        return (c, f, (t + d) % 8)

    def remote(src, dst, sems, index, peer):
        return pltpu.make_async_remote_copy(
            src_ref=src,
            dst_ref=dst,
            send_sem=sems.at[(0,) + index],
            recv_sem=sems.at[(1,) + index],
            device_id=peer,
            device_id_type=MESH,
        )

    def load(src, dst, n):
        return pltpu.make_async_copy(src, dst, load_sem.at[n])

    def li_load(j):
        core = other_c if j % 2 == 0 else c
        column = pl.multiple_of(core * 2560 + order[j // 2] * CHUNK, 128)
        return load(li_hbm.at[:, pl.ds(column, CHUNK)], li.at[j], j)

    cot_load = load(cot_hbm, cot, 8)
    part_rows = VOCAB_OWN // 2
    table_parts = [pl.ds(n * part_rows, part_rows) for n in range(2)]
    table_loads = [
        load(table_hbm.at[rows], table.at[rows], n) for rows, n in zip(table_parts, (9, 21))
    ]
    w_loads = [load(ref, wm.at[n], 10 + n) for n, ref in enumerate((w_hbm, m_hbm, v_hbm))]
    qw_load = load(qw_hbm, qw, 13)
    cache_load = load(cache_hbm, cache, 14)

    small_loads = [load(ids_hbm, ids, 15), load(len_hbm, len_ref, 16), load(gain_hbm, gain, 17)]

    cot_load.start()
    for one in small_loads:
        one.start()
    for one in table_loads:
        one.start()
    for j in range(8):
        li_load(j).start()

    barrier = pltpu.get_barrier_semaphore()
    for d in range(1, 16):
        pl.semaphore_signal(barrier, inc=1, device_id=gf_peer(d), device_id_type=MESH)
    for d in range(1, 8):
        pl.semaphore_signal(barrier, inc=1, device_id=tp_peer(d), device_id_type=MESH)

    cot_load.wait()
    cotf[...] = cot[...].astype(F32)
    for n in range(2):
        cot_t[pl.ds(n * HEAD, HEAD), :] = cotf[pl.ds(n, TOK, 2), :].T.astype(BF16)

    def term(j):
        li_load(j).wait()
        return jnp.dot(cot_t[...], li[j], preferred_element_type=F32).T

    def core_copy(i):
        return remote(core_send.at[i], core_recv.at[i], core_sem, (i,), core_peer)

    def terms(i):
        core_send[i] = term(2 * i).astype(BF16)
        if i == 0:
            pl.semaphore_wait(barrier, 22)
        core_copy(i).start()
        if i == 0:
            for d in range(1, 16):
                e1(d).start()
        own[i] = term(2 * i + 1)

    def add_cores(i):
        core_copy(i).wait_recv()
        for ab in range(2):
            lanes = pl.ds(ab * HEAD, HEAD)
            part[i, ab] = (own[i, :, lanes] + core_recv[i, :, lanes].astype(F32)).astype(BF16)

    def half(way):
        return pl.ds(pl.multiple_of((1 - h if way == 0 else h) * OWN, 64), OWN)

    peers = (a_peer, b_peer)

    def step1(i, ab, slot, way):
        return remote(
            part.at[i, ab, half(way)], recv1.at[ab, slot, way], s1_sem, (ab, slot, way), peers[ab]
        )

    def step2(ab, way):
        return remote(
            send2.at[ab, way], recv2.at[ab, way], s2_sem, (ab, way), peers[1 - ab]
        )

    def step2_go(way):
        for ab, i in ((0, 2), (1, 1)):
            step1(i, ab, 0, way).wait_recv()
            send2[ab, way] = (
                part[i, ab, half(way)].astype(F32) + recv1[ab, 0, way].astype(F32)
            ).astype(BF16)
            step2(ab, way).start()

    def step3(ab):
        return remote(send3.at[ab], recv3.at[ab], s3_sem, (ab,), h_peer)

    def x_sum(ab, way):
        step1(3, ab, 1, way).wait_recv()
        step2(ab, way).wait_recv()
        return (
            part[3, ab, half(way)].astype(F32)
            + recv1[ab, 1, way].astype(F32)
            + recv2[ab, way].astype(F32)
        )

    for one in small_loads:
        one.wait()
    slot = lax.broadcasted_iota(jnp.int32, (16 * PAD, 32), 0)
    row = lax.broadcasted_iota(jnp.int32, (16 * PAD, 32), 1)
    place = slot % PAD
    mine = row == 2 * (slot // PAD) + place % 2
    wanted = jnp.zeros((16 * PAD, 32), F32)
    for step in range(STEPS):
        here = mine & (place // 2 == step)
        wanted = wanted + jnp.where(here, ids[step : step + 1, :].astype(F32), 0.0)
    wanted = jnp.sum(wanted, axis=-1, keepdims=True).astype(jnp.int32)
    wanted = jnp.where(place[:, :1] < 2 * STEPS, wanted, -1)
    hot = jnp.where(
        lax.broadcasted_iota(jnp.int32, (16 * PAD, VOCAB_OWN), 1) == wanted - gf * VOCAB_OWN, 1.0, 0.0
    ).astype(BF16)
    picked = jnp.zeros((16 * PAD, CHUNK), F32)
    for n in range(2):
        table_loads[n].wait()
        columns = slice(n * part_rows, (n + 1) * part_rows)
        picked = picked + jnp.dot(
            hot[:, columns], table[table_parts[n], :], preferred_element_type=F32
        )
    e1_pack[...] = jnp.zeros_like(e1_pack)
    for device in range(16):
        for b in range(5):
            e1_pack[device, b * TOKENS : (b + 1) * TOKENS, :] = picked[
                device * PAD : device * PAD + TOKENS, b * HEAD : (b + 1) * HEAD
            ]
    e1_send[...] = e1_pack[...].astype(BF16)

    def e1(d):
        return remote(e1_send.at[(gf + d) % 16], e1_recv.at[d], e1_sem, (d,), gf_peer(d))

    terms(0)
    qw_load.start()
    terms(1)
    add_cores(0)
    step1(0, 0, 0, 0).start()
    step1(0, 1, 0, 0).start()
    cache_load.start()
    for one in w_loads:
        one.start()
    terms(2)
    add_cores(1)
    step1(1, 0, 1, 0).start()
    terms(3)
    add_cores(2)
    step1(2, 1, 1, 0).start()
    add_cores(3)

    total = e1_send[gf].astype(F32)
    for d in range(1, 16):
        e1(d).wait_recv()
        total = total + e1_recv[d].astype(F32)
    e2[t] = total.astype(BF16)

    def e2_copy(d):
        return remote(e2.at[t], e2.at[t], e2_sem, (d,), tp_peer(d))

    def e2_arrival(d):
        there = (t + 8 - d) % 8
        return remote(e2.at[there], e2.at[there], e2_sem, (d,), tp_peer(d))

    for d in range(1, 8):
        e2_copy(d).start()

    def e3(d, a):
        source = (t + 8 - d) % 8
        to = 2 * source + (h + a) % 2
        return pltpu.make_async_remote_copy(
            src_ref=e2.at[source],
            dst_ref=e3_recv.at[gf],
            send_sem=e3_sem.at[0, 2 * d + a],
            recv_sem=e3_sem.at[1, gf],
            device_id=(to // 8, to % 8, t),
            device_id_type=MESH,
        )

    def e3_arrival(d):
        there = (gf + d) % 16
        return pltpu.make_async_remote_copy(
            src_ref=e2.at[0],
            dst_ref=e3_recv.at[there],
            send_sem=e3_sem.at[0, 0],
            recv_sem=e3_sem.at[1, there],
            device_id=gf_peer(d),
            device_id_type=MESH,
        )

    def itself(d):
        return (t + 8 - d) % 8 == gf // 2

    def e3_go(d):
        e3(d, 1).start()

        @pl.when(jnp.logical_not(itself(d)))
        def _():
            e3(d, 0).start()

        @pl.when(itself(d))
        def _():
            e3_recv[gf] = e2[gf // 2]

    e3_go(0)
    step2_go(0)
    step1(0, 0, 0, 1).start()
    step1(0, 1, 0, 1).start()
    step1(1, 0, 1, 1).start()
    step1(2, 1, 1, 1).start()
    gain32[...] = gain[...].astype(F32)
    fresh[...] = jnp.zeros_like(fresh)
    for ab in range(2):
        send3[ab] = x_sum(ab, 0).astype(BF16)
        step3(ab).start()
    for d in (2, 6, 1, 7, 4, 3, 5):
        e2_arrival(d).wait_recv()
        e3_go(d)
    step2_go(1)
    for n in range(8):
        e2_wide[n] = e2[n].astype(F32)
    square = jnp.zeros((PAD, HEAD), F32)
    for n in range(8):
        for b in range(5):
            one = e2_wide[n, pl.ds(b * TOKENS, PAD), :]
            square = square + one * one
    mean = jnp.sum(square, axis=-1, keepdims=True) * (1.0 / WIDTH)
    factor = lax.rsqrt(mean + norm_eps)
    for n in range(8):
        for b in range(5):
            k = n * 5 + b
            one = e2_wide[n, pl.ds(b * TOKENS, PAD), :] * gain32[k : k + 1, :] * factor
            scaled[:, k * HEAD : (k + 1) * HEAD] = one

    qw_load.wait()
    scaled16 = scaled[...].astype(BF16)

    @pl.loop(0, 4)
    def _(n):
        columns = pl.ds(pl.multiple_of(n * 256, 256), 256)
        qraw[:, columns] = jnp.dot(scaled16, qw[:, columns], preferred_element_type=F32)

    place = lax.broadcasted_iota(jnp.int32, (PAD, HEAD), 0)
    lane = lax.broadcasted_iota(jnp.int32, (PAD, HEAD), 1)
    position = jnp.where(place % 2 == 0, len_ref[0], len_ref[1]) + place // 2
    freqs = jnp.exp((lane % (HEAD // 2)).astype(F32) * (-rope_log * 2.0 / HEAD))
    angles = position.astype(F32) * freqs
    cosine, sine = jnp.cos(angles), jnp.sin(angles)
    sine = jnp.where(lane < HEAD // 2, -sine, sine)

    def rotate(values):
        return values * cosine + pltpu.roll(values, HEAD // 2, 1) * sine

    query = jnp.concatenate(
        [
            rotate(head_norm(qraw[:, g * HEAD : (g + 1) * HEAD]))
            for g in range(HEADS)
        ],
        axis=0,
    ).astype(BF16)

    scale = 1.0 / math.sqrt(HEAD)
    block = 1024

    def attend(r):
        length = len_ref[r]

        def step(n, carry):
            denom, numer = carry
            where = pl.ds(pl.multiple_of(n * block, block), block)
            scores = lax.dot_general(
                query, cache[0, r, where, :], (((1,), (1,)), ((), ())), preferred_element_type=F32
            )
            position = lax.broadcasted_iota(jnp.int32, scores.shape, 1) + n * block
            weights = jnp.where(position < length, jnp.exp(scores * scale), 0.0)
            denom = denom + jnp.sum(weights, axis=-1, keepdims=True)
            numer = numer + jnp.dot(
                weights.astype(BF16), cache[1, r, where, :], preferred_element_type=F32
            )
            return denom, numer

        rows = HEADS * PAD
        return lax.fori_loop(
            0,
            POSITIONS // block,
            step,
            (jnp.zeros((rows, 1), F32), jnp.zeros((rows, HEAD), F32)),
        )

    cache_load.wait()
    first_sums = attend(0)

    for d in range(1, 16):
        e3_arrival(d).wait_recv()
    e3_wide[...] = e3_recv[...].astype(F32)
    first = (gf // 2) * 5 + 2 * h
    columns = []
    for b in range(3):
        low, high = [
            jnp.concatenate(
                [e3_wide[n, pl.ds((b + start) * TOKENS, PAD), :] for n in range(16)], axis=0
            )
            for start in (0, 2)
        ]
        columns.append(jnp.where(h == 0, low, high) * gain32[pl.ds(first + b, 1), :])
    features = jnp.concatenate(columns, axis=1).astype(BF16)

    for one in w_loads:
        one.wait()
    for ab in range(2):
        total = x_sum(ab, 1)
        step3(ab).wait_recv()
        total = total + recv3[ab].astype(F32)
        every = pl.ds(ab, OWN, 2)
        new_weight, new_moment, new_second = adam(
            wm[0, every, :], wm[1, every, :], wm[2, every, :], total
        )
        updated[0, every, :] = new_weight
        updated[1, every, :] = new_moment
        updated[2, every, :] = new_second
        fresh[pl.ds(pl.multiple_of(h * 64, 64), OWN), pl.ds(ab * HEAD, HEAD)] = new_weight.astype(
            BF16
        )
    partial = jnp.dot(features, fresh[...], preferred_element_type=F32)

    def kv(d):
        return remote(kv_send.at[(gf + d) % 16], kv_recv.at[d], kv_sem, (d,), gf_peer(d))

    for n in range(16):
        rows = partial[n * PAD : (n + 1) * PAD]
        kv_send[n] = jnp.concatenate([rows[:, :HEAD], rows[:, HEAD:]], axis=0).astype(BF16)
    for d in range(1, 16):
        kv(d).start()
    stores = [load(updated.at[n], ref, 18 + n) for n, ref in enumerate((nw_hbm, nm_hbm, nv_hbm))]
    for one in stores:
        one.start()

    second_sums = attend(1)
    token = lax.broadcasted_iota(jnp.int32, (HEADS * PAD, 1), 0) % PAD
    first_row = token % 2 == 0
    denom = jnp.where(first_row, first_sums[0], second_sums[0])
    numer = jnp.where(first_row, first_sums[1], second_sums[1])

    total = kv_send[gf].astype(F32)
    for d in range(1, 16):
        kv(d).wait_recv()
        total = total + kv_recv[d].astype(F32)
    new_key = rotate(head_norm(total[:PAD] * factor)).astype(BF16).astype(F32)
    new_value = (total[PAD:] * factor).astype(BF16).astype(F32)
    kv_ref[0] = new_key
    kv_ref[1] = new_value

    query32 = query.astype(F32)
    for j in range(2 * STEPS):
        score = jnp.sum(query32 * new_key[j : j + 1], axis=-1, keepdims=True) * scale
        seen = (token % 2 == j % 2) & (token >= j)
        weight = jnp.where(seen, jnp.exp(score), 0.0)
        denom = denom + weight
        numer = numer + weight.astype(BF16).astype(F32) * new_value[j : j + 1]
    attended = numer / denom
    for g in range(HEADS):
        att_ref[:, pl.ds(g * HEAD, HEAD)] = attended[g * PAD : (g + 1) * PAD]
    for one in stores:
        one.wait()

    for i in range(4):
        core_copy(i).wait_send()
    for way in range(2):
        for ab in range(2):
            step1(0, ab, 0, way).wait_send()
            step1(1 + ab, ab, 1, way).wait_send()
            step2(ab, way).wait_send()
    for ab in range(2):
        step3(ab).wait_send()
    for d in range(1, 8):
        e2_copy(d).wait_send()
    for d in range(1, 16):
        e1(d).wait_send()
        kv(d).wait_send()
    for d in range(8):
        e3(d, 1).wait_send()

        @pl.when(jnp.logical_not(itself(d)))
        def _(d=d):
            e3(d, 0).wait_send()


def finish(w_in, m_in, v_in, kv_in, att_in, w_out, m_out, v_out, kv_out, att_out, state, kv, att, new_kv, out, sem):
    def copy(src, dst, n):
        return pltpu.make_async_copy(src, dst, sem.at[n])

    loads = [copy(kv_in, kv, 0), copy(att_in, att, 1)]
    moves = [copy(ref, state.at[n], 2 + n) for n, ref in enumerate((w_in, m_in, v_in))]
    stores = [copy(state.at[n], ref, 5 + n) for n, ref in enumerate((w_out, m_out, v_out))]
    for one in loads + moves:
        one.start()
    for one in loads:
        one.wait()
    for s in range(STEPS):
        rows = slice(2 * s, 2 * s + 2)
        out[s] = att[rows, :].astype(BF16)
        for n in range(2):
            new_kv[n, s] = kv[n, rows, :].astype(BF16)
    small = [copy(new_kv, kv_out, 8), copy(out, att_out, 9)]
    for one in small:
        one.start()
    for load, store in zip(moves, stores):
        load.wait()
        store.start()
    for one in small + stores:
        one.wait()


def shards(
    learn_input,
    learn_cotangent,
    weight,
    moment,
    second,
    table,
    gain,
    query_weight,
    cache,
    token_ids,
    lengths,
):
    rows = lengths.shape[0]
    state = [one.reshape(2 * OWN, HEAD) for one in (weight, moment, second)]
    anywhere = pl.BlockSpec(memory_space=pl.ANY)
    vmem = pl.BlockSpec(memory_space=pltpu.VMEM)
    dma = pltpu.SemaphoreType.DMA
    like = jax.ShapeDtypeStruct((2 * OWN, HEAD), F32)
    *updated, kv, att = pl.pallas_call(
        kernel,
        out_shape=(
            like,
            like,
            like,
            jax.ShapeDtypeStruct((2, PAD, HEAD), F32),
            jax.ShapeDtypeStruct((PAD, HEADS * HEAD), F32),
        ),
        in_specs=[anywhere] * 11,
        out_specs=(anywhere,) * 3 + (vmem, vmem),
        scratch_shapes=[
            pltpu.VMEM((8, TOK, CHUNK), BF16),
            pltpu.VMEM((2 * TOK, HEAD), BF16),
            pltpu.VMEM((2 * TOK, HEAD), F32),
            pltpu.VMEM((2 * HEAD, TOK), BF16),
            pltpu.VMEM((3, 2 * OWN, HEAD), F32),
            pltpu.VMEM((VOCAB_OWN, CHUNK), BF16),
            pltpu.VMEM((WIDTH, HEADS * HEAD), BF16),
            pltpu.VMEM((2, 2, POSITIONS, HEAD), BF16),
            pltpu.VMEM((4, CHUNK, 2 * HEAD), BF16),
            pltpu.VMEM((4, CHUNK, 2 * HEAD), BF16),
            pltpu.VMEM((4, CHUNK, 2 * HEAD), F32),
            pltpu.VMEM((4, 2, CHUNK, HEAD), BF16),
            pltpu.VMEM((2, 2, 2, OWN, HEAD), BF16),
            pltpu.VMEM((2, 2, OWN, HEAD), BF16),
            pltpu.VMEM((2, 2, OWN, HEAD), BF16),
            pltpu.VMEM((2, OWN, HEAD), BF16),
            pltpu.VMEM((2, OWN, HEAD), BF16),
            pltpu.VMEM((16, ROWS, HEAD), F32),
            pltpu.VMEM((16, ROWS, HEAD), BF16),
            pltpu.VMEM((16, ROWS, HEAD), BF16),
            pltpu.VMEM((8, ROWS, HEAD), BF16),
            pltpu.VMEM((8, ROWS, HEAD), F32),
            pltpu.VMEM((PAD, WIDTH), F32),
            pltpu.VMEM((PAD, HEADS * HEAD), F32),
            pltpu.VMEM((16, ROWS, HEAD), BF16),
            pltpu.VMEM((16, ROWS, HEAD), F32),
            pltpu.VMEM((3 * HEAD, 2 * HEAD), BF16),
            pltpu.VMEM((16, 2 * PAD, HEAD), BF16),
            pltpu.VMEM((16, 2 * PAD, HEAD), BF16),
            pltpu.VMEM((WIDTH // HEAD, HEAD), BF16),
            pltpu.VMEM((WIDTH // HEAD, HEAD), F32),
            pltpu.VMEM((STEPS, 32), jnp.int32),
            pltpu.SMEM((2,), jnp.int32),
            pltpu.VMEM((3, 2 * OWN, HEAD), F32),
            dma((22,)),
            dma((2, 4)),
            dma((2, 2, 2, 2)),
            dma((2, 2, 2)),
            dma((2, 2)),
            dma((2, 16)),
            dma((2, 8)),
            dma((2, 16)),
            dma((2, 16)),
        ],
        compiler_params=pltpu.CompilerParams(
            collective_id=0, has_side_effects=True, vmem_limit_bytes=60 * 1024 * 1024
        ),
        name="step",
    )(
        learn_input,
        learn_cotangent.reshape(2 * TOK, HEAD),
        *state,
        table,
        gain.reshape(WIDTH // HEAD, HEAD),
        query_weight,
        cache.reshape(2, rows, POSITIONS, HEAD),
        token_ids.T,
        lengths,
    )
    *updated, new_kv, attended = pl.pallas_call(
        finish,
        out_shape=(
            like,
            like,
            like,
            jax.ShapeDtypeStruct((2, STEPS, 2, HEAD), BF16),
            jax.ShapeDtypeStruct((STEPS, 2, HEADS * HEAD), BF16),
        ),
        in_specs=[anywhere] * 5,
        out_specs=(anywhere,) * 5,
        scratch_shapes=[
            pltpu.VMEM((3, 2 * OWN, HEAD), F32),
            pltpu.VMEM((2, PAD, HEAD), F32),
            pltpu.VMEM((PAD, HEADS * HEAD), F32),
            pltpu.VMEM((2, STEPS, 2, HEAD), BF16),
            pltpu.VMEM((STEPS, 2, HEADS * HEAD), BF16),
            dma((10,)),
        ],
        name="finish",
    )(*updated, kv, att)
    new_weight, new_moment, new_second = (one.reshape(OWN, 2, HEAD) for one in updated)
    new_kv = new_kv.transpose(0, 2, 1, 3).reshape(2, rows, 1, STEPS, HEAD)
    attended = attended.transpose(1, 0, 2)
    return new_weight, new_moment, new_second, new_kv, attended


def solution(mesh):
    return jax.shard_map(
        shards,
        mesh=mesh,
        in_specs=(
            P(("group", "fsdp"), None),
            P(("group", "fsdp"), None, "tp"),
            P(("group", "fsdp"), None, "tp"),
            P(("group", "fsdp"), None, "tp"),
            P(("group", "fsdp"), None, "tp"),
            P(("group", "fsdp"), "tp"),
            P(),
            P(None, "tp"),
            P(None, ("group", "fsdp"), "tp", None, None),
            P(),
            P(("group", "fsdp")),
        ),
        out_specs=(
            P(("group", "fsdp"), None, "tp"),
            P(("group", "fsdp"), None, "tp"),
            P(("group", "fsdp"), None, "tp"),
            P(None, ("group", "fsdp"), "tp", None, None),
            P(("group", "fsdp"), None, "tp"),
        ),
        check_vma=False,
    )
```

```python
import math

import jax
import jax.numpy as jnp
from jax import lax
from jax.experimental import pallas as pl
from jax.experimental.pallas import tpu as pltpu
from jax.sharding import PartitionSpec as P

MESH = pl.DeviceIdType.MESH
BF16 = jnp.bfloat16
F32 = jnp.float32

WIDTH = 5120
TOK = 1024
HEAD = 128
HEADS = 8
STEPS = 3
VOCAB_OWN = 4864
POSITIONS = 4096
OWN = 320
CHUNK = 640
TOKENS = 6
PAD = 8
ROWS = 32

learn_rate = 0.002
beta_one = 0.9
beta_two = 0.95
bias_one = 1.0 - 0.9**10
bias_two = 1.0 - 0.95**10
adam_eps = 1e-08
weight_decay = 0.1
norm_eps = 1e-06
rope_log = math.log(1000000.0)


def adam(weight, moment, second, grad):
    new_moment = beta_one * moment + (1.0 - beta_one) * grad
    new_second = beta_two * second + (1.0 - beta_two) * grad * grad
    update = new_moment / bias_one / (jnp.sqrt(new_second / bias_two) + adam_eps)
    new_weight = weight - learn_rate * (update + weight_decay * weight)
    return new_weight, new_moment, new_second


def head_norm(values):
    return values * lax.rsqrt(jnp.mean(values * values, axis=-1, keepdims=True) + norm_eps)


def kernel(
    li_hbm,
    cot_hbm,
    w_hbm,
    m_hbm,
    v_hbm,
    table_hbm,
    gain_hbm,
    qw_hbm,
    cache_hbm,
    ids_hbm,
    len_hbm,
    nw_hbm,
    nm_hbm,
    nv_hbm,
    kv_ref,
    att_ref,
    li,
    cot,
    cotf,
    cot_t,
    wm,
    table,
    qw,
    cache,
    core_send,
    core_recv,
    own,
    part,
    recv1,
    send2,
    recv2,
    send3,
    recv3,
    e1_pack,
    e1_send,
    e1_recv,
    e2,
    e2_wide,
    scaled,
    qraw,
    e3_recv,
    e3_wide,
    fresh,
    kv_send,
    kv_recv,
    gain,
    gain32,
    ids,
    len_ref,
    updated,
    load_sem,
    core_sem,
    s1_sem,
    s2_sem,
    s3_sem,
    e1_sem,
    e2_sem,
    e3_sem,
    kv_sem,
):
    c, f, t = lax.axis_index("group"), lax.axis_index("fsdp"), lax.axis_index("tp")
    x, h = f // 2, f % 2
    gf = c * 8 + f
    other_c = 1 - c
    near_a = x + 1 - 2 * (x % 2)
    near_b = 3 - x
    far = (x + 2) % 4
    order = (far, near_a, near_b, x)

    core_peer = (other_c, f, t)
    a_peer = (c, near_a * 2 + h, t)
    b_peer = (c, near_b * 2 + h, t)
    h_peer = (c, x * 2 + 1 - h, t)

    def gf_peer(d):
        there = (gf + d) % 16
        return (there // 8, there % 8, t)

    def tp_peer(d):
        return (c, f, (t + d) % 8)

    def remote(src, dst, sems, index, peer):
        return pltpu.make_async_remote_copy(
            src_ref=src,
            dst_ref=dst,
            send_sem=sems.at[(0,) + index],
            recv_sem=sems.at[(1,) + index],
            device_id=peer,
            device_id_type=MESH,
        )

    def load(src, dst, n):
        return pltpu.make_async_copy(src, dst, load_sem.at[n])

    def li_load(j):
        core = other_c if j % 2 == 0 else c
        column = pl.multiple_of(core * 2560 + order[j // 2] * CHUNK, 128)
        return load(li_hbm.at[:, pl.ds(column, CHUNK)], li.at[j], j)

    cot_load = load(cot_hbm, cot, 8)
    part_rows = VOCAB_OWN // 2
    table_parts = [pl.ds(n * part_rows, part_rows) for n in range(2)]
    table_loads = [
        load(table_hbm.at[rows], table.at[rows], n) for rows, n in zip(table_parts, (9, 21))
    ]
    w_loads = [load(ref, wm.at[n], 10 + n) for n, ref in enumerate((w_hbm, m_hbm, v_hbm))]
    qw_load = load(qw_hbm, qw, 13)
    cache_load = load(cache_hbm, cache, 14)

    small_loads = [load(ids_hbm, ids, 15), load(len_hbm, len_ref, 16), load(gain_hbm, gain, 17)]

    cot_load.start()
    for one in small_loads:
        one.start()
    for one in table_loads:
        one.start()
    for j in range(8):
        li_load(j).start()

    barrier = pltpu.get_barrier_semaphore()
    for d in range(1, 16):
        pl.semaphore_signal(barrier, inc=1, device_id=gf_peer(d), device_id_type=MESH)
    for d in range(1, 8):
        pl.semaphore_signal(barrier, inc=1, device_id=tp_peer(d), device_id_type=MESH)

    cot_load.wait()
    cotf[...] = cot[...].astype(F32)
    for n in range(2):
        cot_t[pl.ds(n * HEAD, HEAD), :] = cotf[pl.ds(n, TOK, 2), :].T.astype(BF16)

    def term(j):
        li_load(j).wait()
        return jnp.dot(cot_t[...], li[j], preferred_element_type=F32).T

    def core_copy(i):
        return remote(core_send.at[i], core_recv.at[i], core_sem, (i,), core_peer)

    def terms(i):
        core_send[i] = term(2 * i).astype(BF16)
        if i == 0:
            pl.semaphore_wait(barrier, 22)
        core_copy(i).start()
        if i == 0:
            for d in range(1, 16):
                e1(d).start()
        own[i] = term(2 * i + 1)

    def add_cores(i):
        core_copy(i).wait_recv()
        for ab in range(2):
            lanes = pl.ds(ab * HEAD, HEAD)
            part[i, ab] = (own[i, :, lanes] + core_recv[i, :, lanes].astype(F32)).astype(BF16)

    def half(way):
        return pl.ds(pl.multiple_of((1 - h if way == 0 else h) * OWN, 64), OWN)

    peers = (a_peer, b_peer)

    def step1(i, ab, slot, way):
        return remote(
            part.at[i, ab, half(way)], recv1.at[ab, slot, way], s1_sem, (ab, slot, way), peers[ab]
        )

    def step2(ab, way):
        return remote(
            send2.at[ab, way], recv2.at[ab, way], s2_sem, (ab, way), peers[1 - ab]
        )

    def step2_go(way):
        for ab, i in ((0, 2), (1, 1)):
            step1(i, ab, 0, way).wait_recv()
            send2[ab, way] = (
                part[i, ab, half(way)].astype(F32) + recv1[ab, 0, way].astype(F32)
            ).astype(BF16)
            step2(ab, way).start()

    def step3(ab):
        return remote(send3.at[ab], recv3.at[ab], s3_sem, (ab,), h_peer)

    def x_sum(ab, way):
        step1(3, ab, 1, way).wait_recv()
        step2(ab, way).wait_recv()
        return (
            part[3, ab, half(way)].astype(F32)
            + recv1[ab, 1, way].astype(F32)
            + recv2[ab, way].astype(F32)
        )

    for one in small_loads:
        one.wait()
    slot = lax.broadcasted_iota(jnp.int32, (16 * PAD, 32), 0)
    row = lax.broadcasted_iota(jnp.int32, (16 * PAD, 32), 1)
    place = slot % PAD
    mine = row == 2 * (slot // PAD) + place % 2
    wanted = jnp.zeros((16 * PAD, 32), F32)
    for step in range(STEPS):
        here = mine & (place // 2 == step)
        wanted = wanted + jnp.where(here, ids[step : step + 1, :].astype(F32), 0.0)
    wanted = jnp.sum(wanted, axis=-1, keepdims=True).astype(jnp.int32)
    wanted = jnp.where(place[:, :1] < 2 * STEPS, wanted, -1)
    hot = jnp.where(
        lax.broadcasted_iota(jnp.int32, (16 * PAD, VOCAB_OWN), 1) == wanted - gf * VOCAB_OWN, 1.0, 0.0
    ).astype(BF16)
    picked = jnp.zeros((16 * PAD, CHUNK), F32)
    for n in range(2):
        table_loads[n].wait()
        columns = slice(n * part_rows, (n + 1) * part_rows)
        picked = picked + jnp.dot(
            hot[:, columns], table[table_parts[n], :], preferred_element_type=F32
        )
    e1_pack[...] = jnp.zeros_like(e1_pack)
    for device in range(16):
        for b in range(5):
            e1_pack[device, b * TOKENS : (b + 1) * TOKENS, :] = picked[
                device * PAD : device * PAD + TOKENS, b * HEAD : (b + 1) * HEAD
            ]
    e1_send[...] = e1_pack[...].astype(BF16)

    def e1(d):
        return remote(e1_send.at[(gf + d) % 16], e1_recv.at[d], e1_sem, (d,), gf_peer(d))

    terms(0)
    qw_load.start()
    terms(1)
    add_cores(0)
    step1(0, 0, 0, 0).start()
    step1(0, 1, 0, 0).start()
    cache_load.start()
    for one in w_loads:
        one.start()
    terms(2)
    add_cores(1)
    step1(1, 0, 1, 0).start()
    terms(3)
    add_cores(2)
    step1(2, 1, 1, 0).start()
    add_cores(3)

    total = e1_send[gf].astype(F32)
    for d in range(1, 16):
        e1(d).wait_recv()
        total = total + e1_recv[d].astype(F32)
    e2[t] = total.astype(BF16)

    def e2_copy(d):
        return remote(e2.at[t], e2.at[t], e2_sem, (d,), tp_peer(d))

    def e2_arrival(d):
        there = (t + 8 - d) % 8
        return remote(e2.at[there], e2.at[there], e2_sem, (d,), tp_peer(d))

    for d in range(1, 8):
        e2_copy(d).start()

    def e3(d, a):
        source = (t + 8 - d) % 8
        to = 2 * source + (h + a) % 2
        return pltpu.make_async_remote_copy(
            src_ref=e2.at[source],
            dst_ref=e3_recv.at[gf],
            send_sem=e3_sem.at[0, 2 * d + a],
            recv_sem=e3_sem.at[1, gf],
            device_id=(to // 8, to % 8, t),
            device_id_type=MESH,
        )

    def e3_arrival(d):
        there = (gf + d) % 16
        return pltpu.make_async_remote_copy(
            src_ref=e2.at[0],
            dst_ref=e3_recv.at[there],
            send_sem=e3_sem.at[0, 0],
            recv_sem=e3_sem.at[1, there],
            device_id=gf_peer(d),
            device_id_type=MESH,
        )

    def itself(d):
        return (t + 8 - d) % 8 == gf // 2

    def e3_go(d):
        e3(d, 1).start()

        @pl.when(jnp.logical_not(itself(d)))
        def _():
            e3(d, 0).start()

        @pl.when(itself(d))
        def _():
            e3_recv[gf] = e2[gf // 2]

    e3_go(0)
    step2_go(0)
    step1(0, 0, 0, 1).start()
    step1(0, 1, 0, 1).start()
    step1(1, 0, 1, 1).start()
    step1(2, 1, 1, 1).start()
    gain32[...] = gain[...].astype(F32)
    fresh[...] = jnp.zeros_like(fresh)
    for ab in range(2):
        send3[ab] = x_sum(ab, 0).astype(BF16)
        step3(ab).start()
    for d in (2, 6, 1, 7, 4, 3, 5):
        e2_arrival(d).wait_recv()
        e3_go(d)
    step2_go(1)
    for n in range(8):
        e2_wide[n] = e2[n].astype(F32)
    square = jnp.zeros((PAD, HEAD), F32)
    for n in range(8):
        for b in range(5):
            one = e2_wide[n, pl.ds(b * TOKENS, PAD), :]
            square = square + one * one
    mean = jnp.sum(square, axis=-1, keepdims=True) * (1.0 / WIDTH)
    factor = lax.rsqrt(mean + norm_eps)
    for n in range(8):
        for b in range(5):
            k = n * 5 + b
            one = e2_wide[n, pl.ds(b * TOKENS, PAD), :] * gain32[k : k + 1, :] * factor
            scaled[:, k * HEAD : (k + 1) * HEAD] = one

    qw_load.wait()
    scaled16 = scaled[...].astype(BF16)

    @pl.loop(0, 4)
    def _(n):
        columns = pl.ds(pl.multiple_of(n * 256, 256), 256)
        qraw[:, columns] = jnp.dot(scaled16, qw[:, columns], preferred_element_type=F32)

    place = lax.broadcasted_iota(jnp.int32, (PAD, HEAD), 0)
    lane = lax.broadcasted_iota(jnp.int32, (PAD, HEAD), 1)
    position = jnp.where(place % 2 == 0, len_ref[0], len_ref[1]) + place // 2
    freqs = jnp.exp((lane % (HEAD // 2)).astype(F32) * (-rope_log * 2.0 / HEAD))
    angles = position.astype(F32) * freqs
    cosine, sine = jnp.cos(angles), jnp.sin(angles)
    sine = jnp.where(lane < HEAD // 2, -sine, sine)

    def rotate(values):
        return values * cosine + pltpu.roll(values, HEAD // 2, 1) * sine

    query = jnp.concatenate(
        [
            rotate(head_norm(qraw[:, g * HEAD : (g + 1) * HEAD]))
            for g in range(HEADS)
        ],
        axis=0,
    ).astype(BF16)

    scale = 1.0 / math.sqrt(HEAD)
    block = 1024

    def attend(r):
        length = len_ref[r]

        def step(n, carry):
            denom, numer = carry
            where = pl.ds(pl.multiple_of(n * block, block), block)
            scores = lax.dot_general(
                query, cache[0, r, where, :], (((1,), (1,)), ((), ())), preferred_element_type=F32
            )
            position = lax.broadcasted_iota(jnp.int32, scores.shape, 1) + n * block
            weights = jnp.where(position < length, jnp.exp(scores * scale), 0.0)
            denom = denom + jnp.sum(weights, axis=-1, keepdims=True)
            numer = numer + jnp.dot(
                weights.astype(BF16), cache[1, r, where, :], preferred_element_type=F32
            )
            return denom, numer

        rows = HEADS * PAD
        return lax.fori_loop(
            0,
            POSITIONS // block,
            step,
            (jnp.zeros((rows, 1), F32), jnp.zeros((rows, HEAD), F32)),
        )

    cache_load.wait()
    first_sums = attend(0)

    for d in range(1, 16):
        e3_arrival(d).wait_recv()
    e3_wide[...] = e3_recv[...].astype(F32)
    first = (gf // 2) * 5 + 2 * h
    columns = []
    for b in range(3):
        low, high = [
            jnp.concatenate(
                [e3_wide[n, pl.ds((b + start) * TOKENS, PAD), :] for n in range(16)], axis=0
            )
            for start in (0, 2)
        ]
        columns.append(jnp.where(h == 0, low, high) * gain32[pl.ds(first + b, 1), :])
    features = jnp.concatenate(columns, axis=1).astype(BF16)

    for one in w_loads:
        one.wait()
    for ab in range(2):
        total = x_sum(ab, 1)
        step3(ab).wait_recv()
        total = total + recv3[ab].astype(F32)
        every = pl.ds(ab, OWN, 2)
        new_weight, _, _ = adam(wm[0, every, :], wm[1, every, :], wm[2, every, :], total)
        updated[0, every, :] = total
        fresh[pl.ds(pl.multiple_of(h * 64, 64), OWN), pl.ds(ab * HEAD, HEAD)] = new_weight.astype(
            BF16
        )
    partial = jnp.dot(features, fresh[...], preferred_element_type=F32)

    def kv(d):
        return remote(kv_send.at[(gf + d) % 16], kv_recv.at[d], kv_sem, (d,), gf_peer(d))

    for n in range(16):
        rows = partial[n * PAD : (n + 1) * PAD]
        kv_send[n] = jnp.concatenate([rows[:, :HEAD], rows[:, HEAD:]], axis=0).astype(BF16)
    for d in range(1, 16):
        kv(d).start()
    updated[0], updated[1], updated[2] = adam(wm[0], wm[1], wm[2], updated[0])
    stores = [load(updated.at[n], ref, 18 + n) for n, ref in enumerate((nw_hbm, nm_hbm, nv_hbm))]
    for one in stores:
        one.start()

    second_sums = attend(1)
    token = lax.broadcasted_iota(jnp.int32, (HEADS * PAD, 1), 0) % PAD
    first_row = token % 2 == 0
    denom = jnp.where(first_row, first_sums[0], second_sums[0])
    numer = jnp.where(first_row, first_sums[1], second_sums[1])

    total = kv_send[gf].astype(F32)
    for d in range(1, 16):
        kv(d).wait_recv()
        total = total + kv_recv[d].astype(F32)
    new_key = rotate(head_norm(total[:PAD] * factor)).astype(BF16).astype(F32)
    new_value = (total[PAD:] * factor).astype(BF16).astype(F32)
    kv_ref[0] = new_key
    kv_ref[1] = new_value

    query32 = query.astype(F32)
    for j in range(2 * STEPS):
        score = jnp.sum(query32 * new_key[j : j + 1], axis=-1, keepdims=True) * scale
        seen = (token % 2 == j % 2) & (token >= j)
        weight = jnp.where(seen, jnp.exp(score), 0.0)
        denom = denom + weight
        numer = numer + weight.astype(BF16).astype(F32) * new_value[j : j + 1]
    attended = numer / denom
    for g in range(HEADS):
        att_ref[:, pl.ds(g * HEAD, HEAD)] = attended[g * PAD : (g + 1) * PAD]
    for one in stores:
        one.wait()

    for i in range(4):
        core_copy(i).wait_send()
    for way in range(2):
        for ab in range(2):
            step1(0, ab, 0, way).wait_send()
            step1(1 + ab, ab, 1, way).wait_send()
            step2(ab, way).wait_send()
    for ab in range(2):
        step3(ab).wait_send()
    for d in range(1, 8):
        e2_copy(d).wait_send()
    for d in range(1, 16):
        e1(d).wait_send()
        kv(d).wait_send()
    for d in range(8):
        e3(d, 1).wait_send()

        @pl.when(jnp.logical_not(itself(d)))
        def _(d=d):
            e3(d, 0).wait_send()


def finish(w_in, m_in, v_in, kv_in, att_in, w_out, m_out, v_out, kv_out, att_out, state, kv, att, new_kv, out, sem):
    def copy(src, dst, n):
        return pltpu.make_async_copy(src, dst, sem.at[n])

    loads = [copy(kv_in, kv, 0), copy(att_in, att, 1)]
    moves = [copy(ref, state.at[n], 2 + n) for n, ref in enumerate((w_in, m_in, v_in))]
    stores = [copy(state.at[n], ref, 5 + n) for n, ref in enumerate((w_out, m_out, v_out))]
    for one in loads + moves:
        one.start()
    for one in loads:
        one.wait()
    for s in range(STEPS):
        rows = slice(2 * s, 2 * s + 2)
        out[s] = att[rows, :].astype(BF16)
        for n in range(2):
            new_kv[n, s] = kv[n, rows, :].astype(BF16)
    small = [copy(new_kv, kv_out, 8), copy(out, att_out, 9)]
    for one in small:
        one.start()
    for load, store in zip(moves, stores):
        load.wait()
        store.start()
    for one in small + stores:
        one.wait()


def shards(
    learn_input,
    learn_cotangent,
    weight,
    moment,
    second,
    table,
    gain,
    query_weight,
    cache,
    token_ids,
    lengths,
):
    rows = lengths.shape[0]
    state = [one.reshape(2 * OWN, HEAD) for one in (weight, moment, second)]
    anywhere = pl.BlockSpec(memory_space=pl.ANY)
    vmem = pl.BlockSpec(memory_space=pltpu.VMEM)
    dma = pltpu.SemaphoreType.DMA
    like = jax.ShapeDtypeStruct((2 * OWN, HEAD), F32)
    *updated, kv, att = pl.pallas_call(
        kernel,
        out_shape=(
            like,
            like,
            like,
            jax.ShapeDtypeStruct((2, PAD, HEAD), F32),
            jax.ShapeDtypeStruct((PAD, HEADS * HEAD), F32),
        ),
        in_specs=[anywhere] * 11,
        out_specs=(anywhere,) * 3 + (vmem, vmem),
        scratch_shapes=[
            pltpu.VMEM((8, TOK, CHUNK), BF16),
            pltpu.VMEM((2 * TOK, HEAD), BF16),
            pltpu.VMEM((2 * TOK, HEAD), F32),
            pltpu.VMEM((2 * HEAD, TOK), BF16),
            pltpu.VMEM((3, 2 * OWN, HEAD), F32),
            pltpu.VMEM((VOCAB_OWN, CHUNK), BF16),
            pltpu.VMEM((WIDTH, HEADS * HEAD), BF16),
            pltpu.VMEM((2, 2, POSITIONS, HEAD), BF16),
            pltpu.VMEM((4, CHUNK, 2 * HEAD), BF16),
            pltpu.VMEM((4, CHUNK, 2 * HEAD), BF16),
            pltpu.VMEM((4, CHUNK, 2 * HEAD), F32),
            pltpu.VMEM((4, 2, CHUNK, HEAD), BF16),
            pltpu.VMEM((2, 2, 2, OWN, HEAD), BF16),
            pltpu.VMEM((2, 2, OWN, HEAD), BF16),
            pltpu.VMEM((2, 2, OWN, HEAD), BF16),
            pltpu.VMEM((2, OWN, HEAD), BF16),
            pltpu.VMEM((2, OWN, HEAD), BF16),
            pltpu.VMEM((16, ROWS, HEAD), F32),
            pltpu.VMEM((16, ROWS, HEAD), BF16),
            pltpu.VMEM((16, ROWS, HEAD), BF16),
            pltpu.VMEM((8, ROWS, HEAD), BF16),
            pltpu.VMEM((8, ROWS, HEAD), F32),
            pltpu.VMEM((PAD, WIDTH), F32),
            pltpu.VMEM((PAD, HEADS * HEAD), F32),
            pltpu.VMEM((16, ROWS, HEAD), BF16),
            pltpu.VMEM((16, ROWS, HEAD), F32),
            pltpu.VMEM((3 * HEAD, 2 * HEAD), BF16),
            pltpu.VMEM((16, 2 * PAD, HEAD), BF16),
            pltpu.VMEM((16, 2 * PAD, HEAD), BF16),
            pltpu.VMEM((WIDTH // HEAD, HEAD), BF16),
            pltpu.VMEM((WIDTH // HEAD, HEAD), F32),
            pltpu.VMEM((STEPS, 32), jnp.int32),
            pltpu.SMEM((2,), jnp.int32),
            pltpu.VMEM((3, 2 * OWN, HEAD), F32),
            dma((22,)),
            dma((2, 4)),
            dma((2, 2, 2, 2)),
            dma((2, 2, 2)),
            dma((2, 2)),
            dma((2, 16)),
            dma((2, 8)),
            dma((2, 16)),
            dma((2, 16)),
        ],
        compiler_params=pltpu.CompilerParams(
            collective_id=0, has_side_effects=True, vmem_limit_bytes=60 * 1024 * 1024
        ),
        name="step",
    )(
        learn_input,
        learn_cotangent.reshape(2 * TOK, HEAD),
        *state,
        table,
        gain.reshape(WIDTH // HEAD, HEAD),
        query_weight,
        cache.reshape(2, rows, POSITIONS, HEAD),
        token_ids.T,
        lengths,
    )
    *updated, new_kv, attended = pl.pallas_call(
        finish,
        out_shape=(
            like,
            like,
            like,
            jax.ShapeDtypeStruct((2, STEPS, 2, HEAD), BF16),
            jax.ShapeDtypeStruct((STEPS, 2, HEADS * HEAD), BF16),
        ),
        in_specs=[anywhere] * 5,
        out_specs=(anywhere,) * 5,
        scratch_shapes=[
            pltpu.VMEM((3, 2 * OWN, HEAD), F32),
            pltpu.VMEM((2, PAD, HEAD), F32),
            pltpu.VMEM((PAD, HEADS * HEAD), F32),
            pltpu.VMEM((2, STEPS, 2, HEAD), BF16),
            pltpu.VMEM((STEPS, 2, HEADS * HEAD), BF16),
            dma((10,)),
        ],
        name="finish",
    )(*updated, kv, att)
    new_weight, new_moment, new_second = (one.reshape(OWN, 2, HEAD) for one in updated)
    new_kv = new_kv.transpose(0, 2, 1, 3).reshape(2, rows, 1, STEPS, HEAD)
    attended = attended.transpose(1, 0, 2)
    return new_weight, new_moment, new_second, new_kv, attended


def solution(mesh):
    return jax.shard_map(
        shards,
        mesh=mesh,
        in_specs=(
            P(("group", "fsdp"), None),
            P(("group", "fsdp"), None, "tp"),
            P(("group", "fsdp"), None, "tp"),
            P(("group", "fsdp"), None, "tp"),
            P(("group", "fsdp"), None, "tp"),
            P(("group", "fsdp"), "tp"),
            P(),
            P(None, "tp"),
            P(None, ("group", "fsdp"), "tp", None, None),
            P(),
            P(("group", "fsdp")),
        ),
        out_specs=(
            P(("group", "fsdp"), None, "tp"),
            P(("group", "fsdp"), None, "tp"),
            P(("group", "fsdp"), None, "tp"),
            P(None, ("group", "fsdp"), "tp", None, None),
            P(("group", "fsdp"), None, "tp"),
        ),
        check_vma=False,
    )
```
